256 devices in a mesh: patch: 32 (over z, y_lo, core), uly: 8 (over y_hi, x).
Axes of the slice: x: 4, y: 4 (y_hi: 2, y_lo: 2; y = y_hi * 2 + y_lo), z: 8, core: 2. Of those that a mesh axis runs over, the one named last changes fastest.
Arguments:
- qkv: bfloat16 [3, 10240, 2048], P(None, ('patch', 'uly')), may hold values from -16 to 16
- stale_kv: bfloat16 [2, 10240, 2048], P(None, 'patch', 'uly'), may hold values from -16 to 16
- out_weight: bfloat16 [2048, 3072], P('uly'), may hold values from -0.125 to 0.125
Outputs:
- mixed: bfloat16 [10240, 3072], P(('patch', 'uly'))
- fresh_kv: bfloat16 [2, 10240, 2048], P(None, 'patch', 'uly')
The draws below stay inside these ranges and needn't reach their ends.
All inputs are finite; a program needn't handle non-finite values.
Results may differ from the reference program's by a relative error of at most 0.018.
Values may be sent and summed in bfloat16 or wider, within the bound.
A program may use at most 128 MiB of HBM per device.

```python
import jax
import jax.numpy as jnp
from jax import lax

D = 3072
HEADS = 16
HEAD_DIM = 128
TOK_GRP = 320
TOKENS = 10240
N_PATCH = 32


def shared_keys(key):
    base = jax.random.normal(key, (TOKENS, HEADS * HEAD_DIM), jnp.float32)
    return jnp.clip(base, -4.0, 4.0)


def draw_qkv(key, part):
    key = jax.random.fold_in(key, 3)
    fresh = jnp.clip(jax.random.normal(key, (3, TOKENS, HEADS * HEAD_DIM), jnp.float32), -4.0, 4.0)
    result = jnp.stack([fresh[0], 3.0 * fresh[1], fresh[2]])
    return result.astype(jnp.bfloat16)


def draw_stale_kv(key, part):
    base = shared_keys(key)
    key = jax.random.fold_in(key, 5)
    values = jnp.clip(jax.random.normal(key, (TOKENS, HEADS * HEAD_DIM), jnp.float32), -4.0, 4.0)
    keys = 3.0 * base
    return jnp.stack([keys, values]).astype(jnp.bfloat16)


def levels(rng, dims, pieces, smallest, largest):
    level, own = 1.0, jax.random.fold_in(rng, 6)
    for dim, shards_of in pieces:
        draws = jnp.exp(jax.random.uniform(jax.random.fold_in(own, dim), (shards_of,), jnp.float32, smallest / len(pieces), largest / len(pieces)))
        level = level * jnp.repeat(draws, dims[dim] // shards_of).reshape([-1 if axis == dim else 1 for axis in range(len(dims))])
    return level


def noise(rng, dims, scale, most, split=(), kind=jnp.bfloat16):
    array = jax.random.normal(rng, dims, jnp.float32) * scale
    if len(split) > 0:
        array = levels(rng, dims, split, -0.22, 0.18) * array
    return jnp.clip(array, min=-most, max=most).astype(kind)


def setup_inputs(seed: int = 0) -> dict:
    streams_of = jax.random.split(jax.random.key(seed), 4)
    qkv = draw_qkv(jax.random.fold_in(streams_of[3], 71), 0)
    stale_kv = draw_stale_kv(jax.random.fold_in(streams_of[3], 71), 0)
    out_weight = noise(streams_of[2], (HEADS * HEAD_DIM, D), (HEADS * HEAD_DIM) ** -0.5, 0.125, ((0, 8),))
    return dict(qkv=qkv, stale_kv=stale_kv, out_weight=out_weight)


def one_head(operands):
    queries, keys, values = operands
    scores = jnp.dot(queries, keys.T, preferred_element_type=jnp.float32) * (HEAD_DIM ** -0.5)
    row_max = jnp.max(scores, axis=1)
    weights = jnp.exp(scores - row_max[:, None])
    row_total = jnp.sum(weights, axis=1)
    probs = weights.astype(jnp.bfloat16)
    summed = jnp.dot(probs, values, preferred_element_type=jnp.float32)
    return (summed / row_total[:, None]).astype(jnp.bfloat16)


def reference(qkv, stale_kv, out_weight):
    def one_group(group_index):
        begin = (group_index * TOK_GRP).astype(jnp.int32)
        fresh_keys = lax.dynamic_slice_in_dim(qkv[1], begin, TOK_GRP, 0)
        fresh_values = lax.dynamic_slice_in_dim(qkv[2], begin, TOK_GRP, 0)
        group_keys = lax.dynamic_update_slice_in_dim(stale_kv[0], fresh_keys, begin, 0)
        group_values = lax.dynamic_update_slice_in_dim(stale_kv[1], fresh_values, begin, 0)
        queries = lax.dynamic_slice_in_dim(qkv[0], begin, TOK_GRP, 0)
        queries = queries.reshape(TOK_GRP, HEADS, HEAD_DIM).transpose(1, 0, 2)
        group_keys = group_keys.reshape(TOKENS, HEADS, HEAD_DIM).transpose(1, 0, 2)
        group_values = group_values.reshape(TOKENS, HEADS, HEAD_DIM).transpose(1, 0, 2)
        heads_out = lax.map(one_head, (queries, group_keys, group_values))
        return heads_out.transpose(1, 0, 2).reshape(TOK_GRP, HEADS * HEAD_DIM)

    attended = lax.map(one_group, jnp.arange(N_PATCH, dtype=jnp.int32))
    attended = attended.reshape(TOKENS, HEADS * HEAD_DIM)
    mixed = jnp.dot(attended, out_weight, preferred_element_type=jnp.float32).astype(jnp.bfloat16)
    return mixed, qkv[1:3]
```

```python
import functools

import jax
import jax.numpy as jnp
from jax import lax
from jax.experimental import pallas as pl
from jax.experimental.pallas import tpu as pltpu
from jax.sharding import PartitionSpec as P

MESH = pl.DeviceIdType.MESH
HD = 128
NZ = 8
NU = 8
TOK = 40
GRP = 320
PAIR = 640
HALF = 160
D = 3072
STEPS = 14
SCALE = HD ** -0.5 * 1.4426950408889634
NT = (((1,), (1,)), ((), ()))
F32 = jnp.float32
BF16 = jnp.bfloat16
W1, W2 = 18, 24
CHUNK = 512


def rows(offset, size, unit=16):
    return pl.ds(pl.multiple_of(offset, unit), size)


def kernel(
    qkv_ref, stale_ref, w_ref, mixed_ref, fresh_ref,
    kv, fr, q, s, p, m, l, acc, qs, kvs, qr, kvr, wg, stat_out, stat_in,
    osend, orecv, bsend, brecv, afin,
    local_sem, ring_s, ring_r, sib_s, sib_r, own_s, own_r, q_s, q_r, f_s, f_r,
    w_s, w_r, wb_s, wb_r, st_s, st_r, o_s, o_r, b_s, b_r,
):
    pi, u = lax.axis_index("patch"), lax.axis_index("uly")
    z, yl, c = pi // 4, (pi // 2) % 2, pi % 2
    yh, x = u // 4, u % 4

    def patch(z_, yl_, c_):
        return z_ * 4 + yl_ * 2 + c_

    sibling = (patch(z, yl, 1 - c), u)
    up = (patch((z + 1) % NZ, yl, c), u)
    down = (patch((z + 7) % NZ, yl, c), u)
    x_up = (pi, yh * 4 + (x + 1) % 4)
    x_down = (pi, yh * 4 + (x + 3) % 4)
    other = patch(z, 1 - yl, c)

    barrier = pltpu.get_barrier_semaphore()
    everyone = [sibling, up, down]
    everyone += [(pi, (u + k) % NU) for k in range(1, NU)]
    everyone += [(other, (u + k) % NU) for k in range(NU)]
    for device in everyone:
        pl.semaphore_signal(barrier, inc=1, device_id=device, device_id_type=MESH)

    def remote(src, dst, send, recv, device):
        return pltpu.make_async_remote_copy(
            src_ref=src, dst_ref=dst, send_sem=send, recv_sem=recv, device_id=device, device_id_type=MESH
        )

    mine = rows(c * GRP, GRP)
    locals_ = []
    for kind in range(4):
        locals_.append(pltpu.make_async_copy(
            stale_ref.at[kind // 2, :, pl.ds(kind % 2 * HD, HD)], kv.at[kind, z, mine, :], local_sem.at[kind]
        ))
    w_local = pltpu.make_async_copy(w_ref, wg.at[rows(x * 2 * HD, 2 * HD), :], local_sem.at[4])
    for copy in locals_:
        copy.start()
    w_local.start()

    for v in range(NU):
        parts = [
            qkv_ref[i, :, pl.ds(v * 2 * HD + h * HD, HD)].astype(F32) for i in range(3) for h in range(2)
        ]
        qs[v] = jnp.concatenate(parts[:2], axis=0).astype(BF16)
        kvs[v] = jnp.concatenate(parts[2:], axis=0).astype(BF16)
    qr[0, u] = qs[u]
    kvr[u] = kvs[u]
    m[...] = jnp.full(m.shape, -jnp.inf, F32)
    l[...] = jnp.zeros(l.shape, F32)
    acc[...] = jnp.zeros(acc.shape, F32)
    for copy in locals_:
        copy.wait()
    w_local.wait()
    pl.semaphore_wait(barrier, len(everyone))

    def part(n, hops_before):
        phase, j = n // STEPS, n % STEPS
        hop, i = j // 4, j % 4
        head, half = i // 2, i % 2
        span = rows(c * GRP + half * HALF, HALF)
        right = kv.at[phase * 2 + head, (z + NZ - hop - hops_before) % NZ, span, :]
        left = kv.at[phase * 2 + 1 - head, (z + hop + hops_before) % NZ, span, :]
        return right, left

    def ring_copies(n, hops_before):
        right, left = part(n, hops_before)
        return (
            remote(right, right, ring_s.at[0, n], ring_r.at[0, n], up),
            remote(left, left, ring_s.at[1, n], ring_r.at[1, n], down),
        )

    def sib_copies(n):
        right, left = part(n, 1)
        return (
            remote(right, right, sib_s.at[0, n], sib_r.at[0, n], sibling),
            remote(left, left, sib_s.at[1, n], sib_r.at[1, n], sibling),
        )

    def sib_wait(n):
        phase, j = n // STEPS, n % STEPS
        hop, i = j // 4, j % 4
        head, half = i // 2, i % 2
        span = rows((1 - c) * GRP + half * HALF, HALF)
        right = kv.at[phase * 2 + head, (z + NZ - hop - 1) % NZ, span, :]
        left = kv.at[phase * 2 + 1 - head, (z + hop + 1) % NZ, span, :]
        remote(right, right, sib_s.at[0, n], sib_r.at[0, n], sibling).wait_recv()
        remote(left, left, sib_s.at[1, n], sib_r.at[1, n], sibling).wait_recv()

    for n in range(4):
        for copy in ring_copies(n, 0):
            copy.start()
    own_sib = remote(kv.at[:, z, mine, :], kv.at[:, z, mine, :], own_s.at[0], own_r.at[0], sibling)
    own_sib.start()

    def q_copies():
        copies = []
        for k in range(1, NU):
            v = (u + k) % NU
            copies.append((remote(qs.at[v], qr.at[0, u], q_s.at[0, k], q_r.at[0, u], (pi, v)), qr.at[0, v], q_r.at[0, v]))
        for k in range(NU):
            v = (u + k) % NU
            copies.append((remote(qs.at[v], qr.at[1, u], q_s.at[1, k], q_r.at[1, u], (other, v)), qr.at[1, v], q_r.at[1, v]))
        return copies

    def f_copies():
        copies = []
        for k in range(1, NU):
            v = (u + k) % NU
            copies.append((remote(kvs.at[v], kvr.at[u], f_s.at[k], f_r.at[u], (pi, v)), kvr.at[v], f_r.at[v]))
        return copies

    for copy, _, _ in q_copies():
        copy.start()

    def w_piece(direction, n):
        if direction == 0:
            origin, half = (x + 3 - n // 2) % 4, n % 2
        else:
            origin, half = (x + 1 + n // 2) % 4, 1 - n % 2
        return origin, half

    def w_slot(origin, half, core):
        return wg.at[rows(origin * 2 * HD + core * HD + half * 64, 64), :]

    def w_send(direction, n):
        if direction == 0:
            slot = w_slot((x + 4 - n // 2) % 4, n % 2, c)
            return remote(slot, slot, w_s.at[0, n], w_r.at[0, n], x_up)
        slot = w_slot((x + n // 2) % 4, 1 - n % 2, c)
        return remote(slot, slot, w_s.at[1, n], w_r.at[1, n], x_down)

    def w_wait(direction, n):
        slot = w_slot(*w_piece(direction, n), c)
        remote(slot, slot, w_s.at[direction, n], w_r.at[direction, n], x_up).wait_recv()

    def w_sib(direction, n, core):
        slot = w_slot(*w_piece(direction, n), core)
        return remote(slot, slot, wb_s.at[direction, n], wb_r.at[direction, n], sibling)

    for n in range(2):
        for direction in range(2):
            w_send(direction, n).start()
    for copy, _, _ in f_copies():
        copy.start()

    def assemble_queries():
        for _, slot, sem in q_copies():
            remote(slot, slot, q_s.at[0, 0], sem, sibling).wait_recv()
        for g in range(2):
            got = [qr[g, v].astype(F32) for v in range(NU)]
            for h in range(2):
                q[h, pl.ds(g * GRP, GRP), :] = jnp.concatenate(
                    [t[h * TOK:(h + 1) * TOK] for t in got], axis=0
                ).astype(BF16)

    def assemble_fresh():
        for _, slot, sem in f_copies():
            remote(slot, slot, f_s.at[0], sem, sibling).wait_recv()
        got = [kvr[v].astype(F32) for v in range(NU)]
        for kind in range(4):
            whole = jnp.concatenate([t[kind * TOK:(kind + 1) * TOK] for t in got], axis=0).astype(BF16)
            fr[kind, mine, :] = whole
            fresh_ref[kind // 2, :, pl.ds(kind % 2 * HD, HD)] = whole
        theirs = rows((1 - c) * GRP, GRP)
        remote(kv.at[:, z, theirs, :], kv.at[:, z, theirs, :], own_s.at[0], own_r.at[0], sibling).wait_recv()
        for kind in range(4):
            fr[kind, theirs, :] = kv[kind, z, theirs, :]

    def note_max(h, span, scores):
        best = m[h, span, :]
        for t in range(PAIR // HD):
            best = jnp.maximum(best, scores[:, t * HD:(t + 1) * HD])
        m[h, span, :] = best

    def score(h, zz):
        scores = lax.dot_general(q[h], kv[h, zz], NT, preferred_element_type=F32)
        s[h, zz] = scores
        note_max(h, slice(None), scores)

    def score_own(h):
        for g, keys in ((0, fr.at[h]), (1, kv.at[h, z])):
            span = pl.ds(g * GRP, GRP)
            scores = lax.dot_general(q[h, span, :], keys[...], NT, preferred_element_type=F32)
            s[h, z, span, :] = scores
            note_max(h, span, scores)

    def weigh(h, zz):
        top, total = m[h], l[h]
        for t in range(PAIR // HD):
            span = pl.ds(t * HD, HD)
            weight = jnp.exp2(s[h, zz, :, span] * SCALE - top)
            total = total + weight
            p[h, zz, :, span] = weight.astype(BF16)
        l[h] = total

    def attend(h, zz):
        acc[h] += jnp.dot(p[h, zz], kv[2 + h, zz], preferred_element_type=F32)

    def attend_own(h):
        for g, values in ((0, fr.at[2 + h]), (1, kv.at[2 + h, z])):
            span = pl.ds(g * GRP, GRP)
            acc[h, span, :] += jnp.dot(p[h, z, span, :], values[...], preferred_element_type=F32)

    def pair(t):
        hop, head = (t - 1) // 2, (t - 1) % 2
        return (z + 7 - hop) % NZ, (z + 1 + hop) % NZ, head

    def pair_arrived(phase, t):
        n = phase * STEPS + 2 * (t - 1)
        sib_wait(n)
        sib_wait(n + 1)

    def score_pair(t):
        pair_arrived(0, t)
        z0, z1, head = pair(t)
        score(head, z0)
        score(1 - head, z1)

    def attend_pair(t):
        pair_arrived(1, t)
        z0, z1, head = pair(t)
        attend(head, z0)
        attend(1 - head, z1)

    def top_of_rows():
        for h in range(2):
            top = jnp.max(m[h], axis=1, keepdims=True) * SCALE
            m[h] = jnp.broadcast_to(top, (PAIR, HD))

    lane = lax.broadcasted_iota(jnp.int32, (PAIR, HD), 1)

    def stat_copy():
        return remote(stat_out, stat_in, st_s.at[0], st_r.at[0], (other, u))

    def send_stats():
        packed = jnp.zeros((PAIR, HD), F32)
        for h in range(2):
            total = jnp.broadcast_to(jnp.sum(l[h], axis=1, keepdims=True), (PAIR, HD))
            l[h] = total
            packed = jnp.where(lane == 2 * h, m[h], packed)
            packed = jnp.where(lane == 2 * h + 1, total, packed)
        stat_out[...] = packed.T[:8]
        stat_copy().start()

    def take_stats():
        stat_copy().wait_recv()
        got = jnp.concatenate([stat_in[...], jnp.zeros((HD - 8, PAIR), F32)], axis=0).T
        got = jnp.concatenate([got[GRP:], got[:GRP]], axis=0)
        for h in range(2):
            top, total = got[:, 2 * h:2 * h + 1], got[:, 2 * h + 1:2 * h + 2]
            mine_top, mine_total = m[h], l[h]
            most = jnp.maximum(mine_top, top)
            own = jnp.exp2(mine_top - most)
            l[h] = own / (mine_total * own + total * jnp.exp2(top - most))

    def body(n, _):
        for direction in range(2):
            arrived = ring_copies(n, 1)[direction]
            arrived.wait_recv()

            @pl.when(n + 4 < 2 * STEPS)
            def _():
                ring_copies(n + 4, 0)[direction].start()

            sib_copies(n)[direction].start()

        @pl.when(n == 4)
        def _():
            assemble_queries()

        @pl.when(n == 5)
        def _():
            assemble_fresh()
            lax.fori_loop(0, 2, lambda h, _: (score_own(h), 0)[1], 0)

        @pl.when(((n >= 6) & (n <= 9)) | (n == 11) | (n == 13) | (n == 15))
        def _():
            score_pair(jnp.where(n <= 9, n - 5, (n - 1) // 2))

        @pl.when(n == 16)
        def _():
            top_of_rows()

        @pl.when((n >= 16) & (n <= 19))
        def _():
            def one(k, _):
                weigh(k % 2, (n - 16) * 2 + k // 2)
                return 0

            lax.fori_loop(0, 4, one, 0)

        @pl.when(n == 19)
        def _():
            send_stats()

        @pl.when(n == 20)
        def _():
            lax.fori_loop(0, 2, lambda h, _: (attend_own(h), 0)[1], 0)

        @pl.when((n >= 21) & (n <= 25) | (n == 27))
        def _():
            attend_pair(jnp.where(n <= 25, n - 20, 6))

        @pl.when(n == W1)
        def _():
            for direction in range(2):
                w_wait(direction, 0)
                w_send(direction, 2).start()
                w_sib(direction, 0, c).start()

        @pl.when(n == W2)
        def _():
            for direction in range(2):
                w_wait(direction, 1)
                w_sib(direction, 1, c).start()

        @pl.when(n == 26)
        def _():
            take_stats()

        return 0

    lax.fori_loop(0, 2 * STEPS, body, 0)
    attend_pair(jnp.int32(7))

    for h in range(2):
        acc[h] = acc[h] * l[h]

    def o_block(same, xt):
        mine_rows, other_rows = (0, GRP) if same else (GRP, 0)
        a = mine_rows + TOK * (4 * yh + xt)
        b = other_rows + TOK * (4 * (1 - yh) + xt)
        return jnp.concatenate(
            [acc[h, rows(r, TOK, 8), :] for r in (a, b) for h in range(2)], axis=0
        ).astype(BF16)

    def o_copy(same, dx):
        xt = (x + dx) % 4
        k = (0 if same else 4) + dx
        return remote(
            osend.at[k], orecv.at[yl * 4 + x], o_s.at[k], o_r.at[yl * 4 + x],
            (pi if same else other, yh * 4 + xt),
        )

    order = [(False, 2), (True, 2), (False, 1), (False, 3), (True, 1), (True, 3), (False, 0)]
    for same, dx in order:
        k = (0 if same else 4) + dx
        osend[k] = o_block(same, (x + dx) % 4)
        o_copy(same, dx).start()
    orecv[yl * 4 + x] = o_block(True, x)

    for direction in range(2):
        w_wait(direction, 2)
        w_sib(direction, 2, c).start()
    for direction in range(2):
        for n in range(3):
            w_sib(direction, n, 1 - c).wait_recv()

    for same, dx in order:
        slot = (yl if same else 1 - yl) * 4 + (x + dx) % 4
        remote(orecv.at[slot], orecv.at[slot], o_s.at[0], o_r.at[slot], sibling).wait_recv()
    columns = []
    for sx in range(4):
        both = orecv[sx].astype(F32) + orecv[4 + sx].astype(F32)
        for h in range(2):
            columns.append(jnp.concatenate(
                [both[h * TOK:(h + 1) * TOK], both[(2 + h) * TOK:(3 + h) * TOK]], axis=0
            ))
    attended = jnp.concatenate(columns, axis=1).astype(BF16)

    facing = (other, (1 - yh) * 4 + x)

    def b_copy(n):
        span = pl.ds(n * HALF, HALF)
        return remote(bsend.at[span, :], brecv.at[span, :], b_s.at[n], b_r.at[n], facing)

    for n in range(D // CHUNK):
        got = jnp.dot(attended, wg[:, pl.ds(n * CHUNK, CHUNK)], preferred_element_type=F32)
        bsend[pl.ds(n * HALF, HALF), :] = jnp.concatenate(
            [got[TOK:, t * HD:(t + 1) * HD] for t in range(CHUNK // HD)], axis=0
        ).astype(BF16)
        b_copy(n).start()
        afin[:, pl.ds(n * CHUNK, CHUNK)] = got[:TOK]
    for n in range(D // CHUNK):
        b_copy(n).wait_recv()
        theirs = brecv[pl.ds(n * HALF, HALF), :].astype(F32)
        theirs = jnp.concatenate([theirs[t * TOK:(t + 1) * TOK] for t in range(CHUNK // HD)], axis=1)
        span = pl.ds(n * CHUNK, CHUNK)
        mixed_ref[:, span] = (afin[:, span] + theirs).astype(BF16)

    def sent(n, _):
        for copy in ring_copies(n, 0) + sib_copies(n):
            copy.wait_send()
        return 0

    lax.fori_loop(0, 2 * STEPS, sent, 0)
    own_sib.wait_send()
    for copy, _, _ in q_copies() + f_copies():
        copy.wait_send()
    for direction in range(2):
        for n in range(3):
            w_send(direction, n).wait_send()
            w_sib(direction, n, c).wait_send()
    stat_copy().wait_send()
    for same, dx in order:
        o_copy(same, dx).wait_send()
    for n in range(D // CHUNK):
        b_copy(n).wait_send()


def on_device(qkv, stale_kv, out_weight):
    vmem = pl.BlockSpec(memory_space=pltpu.VMEM)
    dma = pltpu.SemaphoreType.DMA
    return pl.pallas_call(
        kernel,
        out_shape=(
            jax.ShapeDtypeStruct((TOK, D), BF16),
            jax.ShapeDtypeStruct((2, GRP, 2 * HD), BF16),
        ),
        in_specs=[vmem, vmem, pl.BlockSpec(memory_space=pl.ANY)],
        out_specs=(vmem, vmem),
        scratch_shapes=[
            pltpu.VMEM((4, NZ, PAIR, HD), BF16),
            pltpu.VMEM((4, PAIR, HD), BF16),
            pltpu.VMEM((2, PAIR, HD), BF16),
            pltpu.VMEM((2, NZ, PAIR, PAIR), F32),
            pltpu.VMEM((2, NZ, PAIR, PAIR), BF16),
            pltpu.VMEM((2, PAIR, HD), F32),
            pltpu.VMEM((2, PAIR, HD), F32),
            pltpu.VMEM((2, PAIR, HD), F32),
            pltpu.VMEM((NU, 2 * TOK, HD), BF16),
            pltpu.VMEM((NU, 4 * TOK, HD), BF16),
            pltpu.VMEM((2, NU, 2 * TOK, HD), BF16),
            pltpu.VMEM((NU, 4 * TOK, HD), BF16),
            pltpu.VMEM((8 * HD, D), BF16),
            pltpu.VMEM((8, PAIR), F32),
            pltpu.VMEM((8, PAIR), F32),
            pltpu.VMEM((8, 4 * TOK, HD), BF16),
            pltpu.VMEM((8, 4 * TOK, HD), BF16),
            pltpu.VMEM((TOK * D // HD, HD), BF16),
            pltpu.VMEM((TOK * D // HD, HD), BF16),
            pltpu.VMEM((TOK, D), F32),
            dma((5,)),
            dma((2, 2 * STEPS)), dma((2, 2 * STEPS)), dma((2, 2 * STEPS)), dma((2, 2 * STEPS)),
            dma((1,)), dma((1,)),
            dma((2, NU)), dma((2, NU)), dma((NU,)), dma((NU,)),
            dma((2, 3)), dma((2, 3)), dma((2, 3)), dma((2, 3)),
            dma((1,)), dma((1,)),
            dma((8,)), dma((8,)), dma((D // CHUNK,)), dma((D // CHUNK,)),
        ],
        compiler_params=pltpu.CompilerParams(
            collective_id=0, has_side_effects=True, vmem_limit_bytes=62 * 2**20
        ),
    )(qkv, stale_kv, out_weight)


def solution(mesh):
    placed = (P(None, ("patch", "uly"), None), P(None, "patch", "uly"), P("uly", None))
    return jax.shard_map(
        on_device,
        mesh=mesh,
        in_specs=placed,
        out_specs=(P(("patch", "uly"), None), P(None, "patch", "uly")),
        check_vma=False,
    )
```

```python
import functools

import jax
import jax.numpy as jnp
from jax import lax
from jax.experimental import pallas as pl
from jax.experimental.pallas import tpu as pltpu
from jax.sharding import PartitionSpec as P

MESH = pl.DeviceIdType.MESH
HD = 128
NZ = 8
NU = 8
TOK = 40
GRP = 320
PAIR = 640
HALF = 160
D = 3072
STEPS = 14
SCALE = HD ** -0.5 * 1.4426950408889634
NT = (((1,), (1,)), ((), ()))
F32 = jnp.float32
BF16 = jnp.bfloat16
W1, W2 = 13, 23
CHUNK = 512


def rows(offset, size, unit=16):
    return pl.ds(pl.multiple_of(offset, unit), size)


def kernel(
    qkv_ref, stale_ref, w_ref, mixed_ref, fresh_ref,
    qkv, kv, fr, q, s, p, m, top, fix, l, acc, qs, kvs, qr, kvr, wg, stat_out, stat_in,
    osend, orecv, bsend, brecv, afin, mixed, fresh,
    local_sem, ring_r, pass_s, sib_r, own_s, own_r, q_s, q_r, f_s, f_r,
    w_s, w_r, wb_r, st_s, st_r, o_s, o_r, b_s, b_r,
):
    pi, u = lax.axis_index("patch"), lax.axis_index("uly")
    z, yl, c = pi // 4, (pi // 2) % 2, pi % 2
    yh, x = u // 4, u % 4

    def patch(z_, yl_, c_):
        return z_ * 4 + yl_ * 2 + c_

    sibling = (patch(z, yl, 1 - c), u)
    up = (patch((z + 1) % NZ, yl, c), u)
    down = (patch((z + 7) % NZ, yl, c), u)
    x_up = (pi, yh * 4 + (x + 1) % 4)
    x_down = (pi, yh * 4 + (x + 3) % 4)
    other = patch(z, 1 - yl, c)

    barrier = pltpu.get_barrier_semaphore()
    everyone = [sibling, up, down]
    everyone += [(pi, (u + k) % NU) for k in range(1, NU)]
    everyone += [(other, (u + k) % NU) for k in range(NU)]
    for device in everyone:
        pl.semaphore_signal(barrier, inc=1, device_id=device, device_id_type=MESH)

    def remote(src, dst, send, recv, device):
        return pltpu.make_async_remote_copy(
            src_ref=src, dst_ref=dst, send_sem=send, recv_sem=recv, device_id=device, device_id_type=MESH
        )

    mine = rows(c * GRP, GRP)
    def wait(ref, sem):
        pltpu.make_async_copy(ref, ref, sem).wait()

    qkv_in = pltpu.make_async_copy(qkv_ref, qkv, local_sem.at[7])
    qkv_in.start()
    locals_ = []
    for kind in range(4):
        locals_.append(pltpu.make_async_copy(
            stale_ref.at[kind // 2, :, pl.ds(kind % 2 * HD, HD)], kv.at[kind, z, mine, :], local_sem.at[kind]
        ))
    w_local = pltpu.make_async_copy(w_ref, wg.at[rows(x * 2 * HD, 2 * HD), :], local_sem.at[4])
    for copy in locals_:
        copy.start()
    w_local.start()

    qkv_in.wait()
    for v in range(NU):
        parts = [
            qkv[i, :, pl.ds(v * 2 * HD + h * HD, HD)].astype(F32) for i in range(3) for h in range(2)
        ]
        qs[v] = jnp.concatenate(parts[:2], axis=0).astype(BF16)
        kvs[v] = jnp.concatenate(parts[2:], axis=0).astype(BF16)
    pltpu.make_async_copy(qs.at[u], qr.at[0, u], q_r.at[0]).start()
    pltpu.make_async_copy(kvs.at[u], kvr.at[u], f_r.at[0]).start()
    m[...] = jnp.full(m.shape, -jnp.inf, F32)
    l[...] = jnp.zeros(l.shape, F32)
    acc[...] = jnp.zeros(acc.shape, F32)
    for copy in locals_:
        copy.wait()
    w_local.wait()
    pl.semaphore_wait(barrier, len(everyone))

    def part(n, hops_before):
        phase, j = n // STEPS, n % STEPS
        hop, i = j // 4, j % 4
        head, half = i // 2, i % 2
        span = rows(c * GRP + half * HALF, HALF)
        right = kv.at[phase * 2 + head, (z + NZ - hop - hops_before) % NZ, span, :]
        left = kv.at[phase * 2 + 1 - head, (z + hop + hops_before) % NZ, span, :]
        return right, left

    def ring_copies(n, hops_before):
        for slot, device in zip(part(n, hops_before), (up, down)):
            yield remote(slot, slot, pass_s.at[0], ring_r.at[n], device)

    def sib_copies(n):
        for slot in part(n, 1):
            yield remote(slot, slot, pass_s.at[0], sib_r.at[n // 2], sibling)

    for n in range(4):
        for copy in ring_copies(n, 0):
            copy.start()
    own_sib = remote(kv.at[:, z, mine, :], kv.at[:, z, mine, :], own_s.at[0], own_r.at[0], sibling)
    own_sib.start()

    def q_copies():
        for g, where in ((0, pi), (1, other)):
            for k in range(1 - g, NU):
                v = (u + k) % NU
                yield remote(qs.at[v], qr.at[g, u], q_s.at[g], q_r.at[0], (where, v))

    def f_copies():
        for k in range(1, NU):
            v = (u + k) % NU
            yield remote(kvs.at[v], kvr.at[u], f_s.at[0], f_r.at[0], (pi, v))

    for copy in q_copies():
        copy.start()
    for copy in f_copies():
        copy.start()

    def w_piece(direction, n):
        if direction == 0:
            origin, half = (x + 3 - n // 2) % 4, n % 2
        else:
            origin, half = (x + 1 + n // 2) % 4, 1 - n % 2
        return origin, half

    def w_slot(origin, half, core):
        return wg.at[rows(origin * 2 * HD + core * HD + half * 64, 64), :]

    def w_send(direction, n):
        if direction == 0:
            slot = w_slot((x + 4 - n // 2) % 4, n % 2, c)
            return remote(slot, slot, w_s.at[0], w_r.at[0, n], x_up)
        slot = w_slot((x + n // 2) % 4, 1 - n % 2, c)
        return remote(slot, slot, w_s.at[0], w_r.at[1, n], x_down)

    def w_wait(direction, n):
        wait(w_slot(*w_piece(direction, n), c), w_r.at[direction, n])

    def w_sib(direction, n):
        slot = w_slot(*w_piece(direction, n), c)
        return remote(slot, slot, w_s.at[0], wb_r.at[0], sibling)

    for n in range(2):
        for direction in range(2):
            w_send(direction, n).start()
    def assemble_queries():
        wait(qr, q_r.at[0])
        for g in range(2):
            got = [qr[g, v].astype(F32) for v in range(NU)]
            for h in range(2):
                q[h, pl.ds(g * GRP, GRP), :] = jnp.concatenate(
                    [t[h * TOK:(h + 1) * TOK] for t in got], axis=0
                ).astype(BF16)

    fresh_out = pltpu.make_async_copy(fresh, fresh_ref, local_sem.at[5])
    mixed_out = pltpu.make_async_copy(mixed, mixed_ref, local_sem.at[6])

    def assemble_fresh():
        wait(kvr, f_r.at[0])
        got = [kvr[v].astype(F32) for v in range(NU)]
        for kind in range(4):
            whole = jnp.concatenate([t[kind * TOK:(kind + 1) * TOK] for t in got], axis=0).astype(BF16)
            fr[kind, mine, :] = whole
            fresh[kind // 2, :, pl.ds(kind % 2 * HD, HD)] = whole
        fresh_out.start()
        theirs = rows((1 - c) * GRP, GRP)
        wait(kv.at[:, z, theirs, :], own_r.at[0])
        for kind in range(4):
            fr[kind, theirs, :] = kv[kind, z, theirs, :]

    def note_max(h, span, scores):
        best = m[h, span, :]
        for t in range(PAIR // HD):
            best = jnp.maximum(best, scores[:, t * HD:(t + 1) * HD])
        m[h, span, :] = best

    def score(h, zz):
        scores = lax.dot_general(q[h], kv[h, zz], NT, preferred_element_type=F32)
        s[h, zz] = scores
        note_max(h, slice(None), scores)

    def score_own(h):
        for g, keys in ((0, fr.at[h]), (1, kv.at[h, z])):
            span = pl.ds(g * GRP, GRP)
            scores = lax.dot_general(q[h, span, :], keys[...], NT, preferred_element_type=F32)
            s[h, z, span, :] = scores
            note_max(h, span, scores)

    def weigh(h, zz):
        most, total = top[h], l[h]
        for t in range(PAIR // HD):
            span = pl.ds(t * HD, HD)
            weight = jnp.exp2(s[h, zz, :, span] * SCALE - most)
            total = total + weight
            p[h, zz, :, span] = weight.astype(BF16)
        l[h] = total

    def attend(h, zz):
        acc[h] += jnp.dot(p[h, zz], kv[2 + h, zz], preferred_element_type=F32)

    def attend_own(h):
        for g, values in ((0, fr.at[2 + h]), (1, kv.at[2 + h, z])):
            span = pl.ds(g * GRP, GRP)
            acc[h, span, :] += jnp.dot(p[h, z, span, :], values[...], preferred_element_type=F32)

    def pair(t):
        hop, head = (t - 1) // 2, (t - 1) % 2
        return (z + 7 - hop) % NZ, (z + 1 + hop) % NZ, head

    def pair_arrived(phase, t):
        wait(kv.at[0, 0], sib_r.at[phase * STEPS // 2 + t - 1])

    def score_pair(t):
        pair_arrived(0, t)
        z0, z1, head = pair(t)
        score(head, z0)
        score(1 - head, z1)

    def attend_pair(t):
        pair_arrived(1, t)
        z0, z1, head = pair(t)
        attend(head, z0)
        attend(1 - head, z1)

    def row_max(h):
        return jnp.broadcast_to(jnp.max(m[h], axis=1, keepdims=True) * SCALE, (PAIR, HD))

    def first_top():
        for h in range(2):
            top[h] = row_max(h)

    def last_top():
        for h in range(2):
            old, new = top[h], row_max(h)
            top[h] = new
            fix[h] = jnp.exp2(old - new)
            l[h] = l[h] * fix[h]

    def weigh_pair(t):
        z0, z1, head = pair(t)
        z0, z1, head = jnp.where(t == 0, z, z0), jnp.where(t == 0, z, z1), jnp.where(t == 0, 0, head)

        def one(k, _):
            weigh(jnp.where(k == 0, head, 1 - head), jnp.where(k == 0, z0, z1))
            return 0

        lax.fori_loop(0, 2, one, 0)

    lane = lax.broadcasted_iota(jnp.int32, (PAIR, HD), 1)

    def stat_copy():
        return remote(stat_out, stat_in, st_s.at[0], st_r.at[0], (other, u))

    def send_stats():
        packed = jnp.zeros((PAIR, HD), F32)
        for h in range(2):
            total = jnp.broadcast_to(jnp.sum(l[h], axis=1, keepdims=True), (PAIR, HD))
            l[h] = total
            packed = jnp.where(lane == 2 * h, top[h], packed)
            packed = jnp.where(lane == 2 * h + 1, total, packed)
        stat_out[...] = packed.T[:8]
        stat_copy().start()

    def take_stats():
        stat_copy().wait_recv()
        got = jnp.concatenate([stat_in[...], jnp.zeros((HD - 8, PAIR), F32)], axis=0).T
        got = jnp.concatenate([got[GRP:], got[:GRP]], axis=0)
        for h in range(2):
            their_top, total = got[:, 2 * h:2 * h + 1], got[:, 2 * h + 1:2 * h + 2]
            mine_top, mine_total = top[h], l[h]
            most = jnp.maximum(mine_top, their_top)
            own = jnp.exp2(mine_top - most)
            l[h] = own / (mine_total * own + total * jnp.exp2(their_top - most))

    def body(n, _):
        wait(kv.at[0, 0, pl.ds(0, GRP), :], ring_r.at[n])

        @pl.when(n + 4 < 2 * STEPS)
        def _():
            for copy in ring_copies(n + 4, 0):
                copy.start()

        for copy in sib_copies(n):
            copy.start()

        @pl.when(n == 2)
        def _():
            assemble_queries()

        @pl.when((n % 2 == 1) & (n >= 3) & (n <= 15))
        def _():
            score_pair((n - 1) // 2)

        @pl.when(n == 6)
        def _():
            assemble_fresh()
            lax.fori_loop(0, 2, lambda h, _: (score_own(h), 0)[1], 0)

        @pl.when(n == 10)
        def _():
            first_top()

        @pl.when(n == 16)
        def _():
            last_top()

        @pl.when(((n % 2 == 0) & (n >= 10) & (n <= 20)) | (n == 21) | (n == 22))
        def _():
            weigh_pair(jnp.where(n <= 20, (n - 10) // 2, n - 15))

        @pl.when(n == 22)
        def _():
            send_stats()

        @pl.when(n == 17)
        def _():
            lax.fori_loop(0, 2, lambda h, _: (attend_own(h), 0)[1], 0)

        @pl.when((n == 19) | (n >= 23))
        def _():
            attend_pair(jnp.where(n == 19, 1, n - 21))

        @pl.when(n == 23)
        def _():
            for h in range(2):
                acc[h] = acc[h] * fix[h]

        @pl.when(n == W1)
        def _():
            for direction in range(2):
                w_wait(direction, 0)
                w_send(direction, 2).start()
                w_sib(direction, 0).start()

        @pl.when(n == W2)
        def _():
            for direction in range(2):
                w_wait(direction, 1)
                w_sib(direction, 1).start()

        return 0

    lax.fori_loop(0, 2 * STEPS, body, 0)
    take_stats()
    attend_pair(jnp.int32(7))

    for h in range(2):
        acc[h] = acc[h] * l[h]

    def o_block(same, xt):
        mine_rows, other_rows = (0, GRP) if same else (GRP, 0)
        a = mine_rows + TOK * (4 * yh + xt)
        b = other_rows + TOK * (4 * (1 - yh) + xt)
        return jnp.concatenate(
            [acc[h, rows(r, TOK, 8), :] for r in (a, b) for h in range(2)], axis=0
        ).astype(BF16)

    def o_copy(same, dx):
        xt = (x + dx) % 4
        k = (0 if same else 4) + dx
        return remote(
            osend.at[k], orecv.at[yl * 4 + x], o_s.at[0], o_r.at[0],
            (pi if same else other, yh * 4 + xt),
        )

    order = [(False, 2), (True, 2), (False, 1), (False, 3), (True, 1), (True, 3), (False, 0)]
    for same, dx in order:
        k = (0 if same else 4) + dx
        osend[k] = o_block(same, (x + dx) % 4)
        o_copy(same, dx).start()
    osend[0] = o_block(True, x)
    pltpu.make_async_copy(osend.at[0], orecv.at[yl * 4 + x], o_r.at[0]).start()

    for direction in range(2):
        w_wait(direction, 2)
        w_sib(direction, 2).start()
    wait(wg.at[pl.ds(0, 3 * HD), :], wb_r.at[0])

    wait(orecv, o_r.at[0])
    columns = []
    for sx in range(4):
        both = orecv[sx].astype(F32) + orecv[4 + sx].astype(F32)
        for h in range(2):
            columns.append(jnp.concatenate(
                [both[h * TOK:(h + 1) * TOK], both[(2 + h) * TOK:(3 + h) * TOK]], axis=0
            ))
    attended = jnp.concatenate(columns, axis=1).astype(BF16)

    facing = (other, (1 - yh) * 4 + x)

    def b_copy(n):
        span = pl.ds(n * HALF, HALF)
        return remote(bsend.at[span, :], brecv.at[span, :], b_s.at[0], b_r.at[n], facing)

    for n in range(D // CHUNK):
        got = jnp.dot(attended, wg[:, pl.ds(n * CHUNK, CHUNK)], preferred_element_type=F32)
        bsend[pl.ds(n * HALF, HALF), :] = jnp.concatenate(
            [got[TOK:, t * HD:(t + 1) * HD] for t in range(CHUNK // HD)], axis=0
        ).astype(BF16)
        b_copy(n).start()
        afin[:, pl.ds(n * CHUNK, CHUNK)] = got[:TOK]
    for n in range(D // CHUNK):
        b_copy(n).wait_recv()
        theirs = brecv[pl.ds(n * HALF, HALF), :].astype(F32)
        theirs = jnp.concatenate([theirs[t * TOK:(t + 1) * TOK] for t in range(CHUNK // HD)], axis=1)
        span = pl.ds(n * CHUNK, CHUNK)
        mixed[:, span] = (afin[:, span] + theirs).astype(BF16)
    mixed_out.start()

    wait(kv.at[:, pl.ds(0, 7)], pass_s.at[0])
    wait(kv.at[:, z, mine, :], own_s.at[0])
    wait(qs.at[pl.ds(1, 7)], q_s.at[0])
    wait(qs, q_s.at[1])
    wait(kvs.at[pl.ds(1, 7)], f_s.at[0])
    wait(wg.at[pl.ds(0, 6 * HD), :], w_s.at[0])
    wait(stat_out, st_s.at[0])
    wait(osend.at[pl.ds(1, 7)], o_s.at[0])
    wait(bsend, b_s.at[0])
    fresh_out.wait()
    mixed_out.wait()


def hand_over(mixed_in, fresh_in, mixed_out, fresh_out):
    mixed_out[...] = mixed_in[...]
    fresh_out[...] = fresh_in[...]


def on_device(qkv, stale_kv, out_weight):
    vmem = pl.BlockSpec(memory_space=pltpu.VMEM)
    dma = pltpu.SemaphoreType.DMA
    anywhere = pl.BlockSpec(memory_space=pl.ANY)
    shapes = (
        jax.ShapeDtypeStruct((TOK, D), BF16),
        jax.ShapeDtypeStruct((2, GRP, 2 * HD), BF16),
    )
    results = pl.pallas_call(
        kernel,
        out_shape=shapes,
        in_specs=[anywhere] * 3,
        out_specs=(anywhere, anywhere),
        scratch_shapes=[
            pltpu.VMEM((3, TOK, NU * 2 * HD), BF16),
            pltpu.VMEM((4, NZ, PAIR, HD), BF16),
            pltpu.VMEM((4, PAIR, HD), BF16),
            pltpu.VMEM((2, PAIR, HD), BF16),
            pltpu.VMEM((2, NZ, PAIR, PAIR), F32),
            pltpu.VMEM((2, NZ, PAIR, PAIR), BF16),
            pltpu.VMEM((2, PAIR, HD), F32),
            pltpu.VMEM((2, PAIR, HD), F32),
            pltpu.VMEM((2, PAIR, HD), F32),
            pltpu.VMEM((2, PAIR, HD), F32),
            pltpu.VMEM((2, PAIR, HD), F32),
            pltpu.VMEM((NU, 2 * TOK, HD), BF16),
            pltpu.VMEM((NU, 4 * TOK, HD), BF16),
            pltpu.VMEM((2, NU, 2 * TOK, HD), BF16),
            pltpu.VMEM((NU, 4 * TOK, HD), BF16),
            pltpu.VMEM((8 * HD, D), BF16),
            pltpu.VMEM((8, PAIR), F32),
            pltpu.VMEM((8, PAIR), F32),
            pltpu.VMEM((8, 4 * TOK, HD), BF16),
            pltpu.VMEM((8, 4 * TOK, HD), BF16),
            pltpu.VMEM((TOK * D // HD, HD), BF16),
            pltpu.VMEM((TOK * D // HD, HD), BF16),
            pltpu.VMEM((TOK, D), F32),
            pltpu.VMEM((TOK, D), BF16),
            pltpu.VMEM((2, GRP, 2 * HD), BF16),
            dma((8,)), dma((2 * STEPS,)), dma((1,)), dma((STEPS,)), dma((1,)), dma((1,)),
            dma((2,)), dma((1,)), dma((1,)), dma((1,)), dma((1,)), dma((2, 3)), dma((1,)),
            dma((1,)), dma((1,)), dma((1,)), dma((1,)), dma((1,)), dma((D // CHUNK,)),
        ],
        compiler_params=pltpu.CompilerParams(
            collective_id=0, has_side_effects=True, vmem_limit_bytes=62 * 2**20
        ),
    )(qkv, stale_kv, out_weight)
    return pl.pallas_call(
        hand_over,
        out_shape=shapes,
        in_specs=[vmem, vmem],
        out_specs=(vmem, vmem),
    )(*results)


def solution(mesh):
    placed = (P(None, ("patch", "uly"), None), P(None, "patch", "uly"), P("uly", None))
    return jax.shard_map(
        on_device,
        mesh=mesh,
        in_specs=placed,
        out_specs=(P(("patch", "uly"), None), P(None, "patch", "uly")),
        check_vma=False,
    )
```

```python
import functools

import jax
import jax.numpy as jnp
from jax import lax
from jax.experimental import pallas as pl
from jax.experimental.pallas import tpu as pltpu
from jax.sharding import PartitionSpec as P

MESH = pl.DeviceIdType.MESH
HD = 128
NZ = 8
NU = 8
TOK = 40
GRP = 320
PAIR = 640
HALF = 160
BAND = 64
OWN = 7 * PAIR
D = 3072
STEPS = 14
SCALE = HD ** -0.5 * 1.4426950408889634
NT = (((1,), (1,)), ((), ()))
F32 = jnp.float32
BF16 = jnp.bfloat16
AHEAD = 6
CHUNK = 512


def rows(offset, size, unit=16):
    return pl.ds(pl.multiple_of(offset, unit), size)


def kernel(
    qkv_ref, stale_ref, w_ref, mine_ref, their_ref, fresh_ref,
    qkv, kv, fr, q, s, p, m, top, fix, l, acc, qs, kvs, qr, kvr, wg, stat_out, stat_in,
    osend, orecv, att, bsend, afin, fresh,
    local_sem, ring_r, pass_s, sib_r, own_s, own_r, q_s, q_r, f_s, f_r,
    w_s, w_r, wb_r, wy_r, st_s, st_r, o_s, o_r, b_s, b_r,
):
    pi, u = lax.axis_index("patch"), lax.axis_index("uly")
    z, yl, c = pi // 4, (pi // 2) % 2, pi % 2
    yh, x = u // 4, u % 4

    def patch(z_, yl_, c_):
        return z_ * 4 + yl_ * 2 + c_

    sibling = (patch(z, yl, 1 - c), u)
    up = (patch((z + 1) % NZ, yl, c), u)
    down = (patch((z + 7) % NZ, yl, c), u)
    x_up = (pi, yh * 4 + (x + 1) % 4)
    x_down = (pi, yh * 4 + (x + 3) % 4)
    other = patch(z, 1 - yl, c)

    barrier = pltpu.get_barrier_semaphore()
    everyone = [sibling, up, down]
    everyone += [(pi, (u + k) % NU) for k in range(1, NU)]
    everyone += [(other, (u + k) % NU) for k in range(NU)]
    for device in everyone:
        pl.semaphore_signal(barrier, inc=1, device_id=device, device_id_type=MESH)

    def remote(src, dst, send, recv, device):
        return pltpu.make_async_remote_copy(
            src_ref=src, dst_ref=dst, send_sem=send, recv_sem=recv, device_id=device, device_id_type=MESH
        )

    mine = rows(OWN + c * GRP, GRP)
    def wait(ref, sem):
        pltpu.make_async_copy(ref, ref, sem).wait()

    qkv_in = pltpu.make_async_copy(qkv_ref, qkv, local_sem.at[7])
    locals_ = []
    for kind in range(4):
        locals_.append(pltpu.make_async_copy(
            stale_ref.at[kind // 2, :, pl.ds(kind % 2 * HD, HD)], kv.at[kind, mine, :], local_sem.at[kind]
        ))
    w_local = pltpu.make_async_copy(w_ref, wg.at[rows(x * 2 * HD, 2 * HD), :], local_sem.at[4])
    for copy in locals_:
        copy.start()
    qkv_in.start()
    w_local.start()

    for copy in locals_:
        copy.wait()
    pl.semaphore_wait(barrier, len(everyone))

    turns = ["Ka0", "Kb0", "Va0", "Ka1", "Kb1", "Vb0", "Ka2", "Kb2", "Va1", "Vb1", "Ka3", "Va2", "Vb2", "Va3"]

    def turn(n):
        phase, head, hop = turns[n // 2]
        return "KV".index(phase), 2 * int(hop) + "ab".index(head)

    def turn_of(phase, i):
        return turns.index("KV"[phase] + "ab"[i % 2] + str(i // 2))

    def place(hops, direction):
        return PAIR * {0: 7, 4: 6}.get(hops, 2 * hops - 2 + direction)

    def ring_copies(n):
        phase, i = turn(n)
        hop, head = i // 2, i % 2
        start = c * GRP + n % 2 * HALF
        for direction, device in ((0, up), (1, down)):
            kind = phase * 2 + (head if direction == 0 else 1 - head)
            yield remote(
                kv.at[kind, rows(place(hop, direction) + start, HALF), :],
                kv.at[kind, rows(place(hop + 1, direction) + start, HALF), :],
                pass_s.at[0], ring_r.at[n], device,
            )

    def sib_copies(n):
        phase, i = turn(n)
        hop, head = i // 2, i % 2
        for direction in range(2):
            kind = phase * 2 + (head if direction == 0 else 1 - head)
            slot = kv.at[kind, rows(place(hop + 1, direction) + c * GRP, GRP), :]
            yield remote(slot, slot, pass_s.at[0], sib_r.at[n // 2], sibling)

    for n in range(AHEAD):
        for copy in ring_copies(n):
            copy.start()
    own_sib = remote(kv.at[:, mine, :], kv.at[:, mine, :], own_s.at[0], own_r.at[0], sibling)
    own_sib.start()

    qkv_in.wait()
    for v in range(NU):
        parts = [
            qkv[i, :, pl.ds(v * 2 * HD + h * HD, HD)].astype(F32) for i in range(3) for h in range(2)
        ]
        qs[v] = jnp.concatenate(parts[:2], axis=0).astype(BF16)
        kvs[v] = jnp.concatenate(parts[2:], axis=0).astype(BF16)
    pltpu.make_async_copy(qs.at[u], qr.at[0, u], q_r.at[0]).start()
    pltpu.make_async_copy(kvs.at[u], kvr.at[u], f_r.at[0]).start()
    m[...] = jnp.full(m.shape, -jnp.inf, F32)
    l[...] = jnp.zeros(l.shape, F32)
    acc[...] = jnp.zeros(acc.shape, F32)

    def q_copies():
        for g, where in ((0, pi), (1, other)):
            for k in range(1 - g, NU):
                v = (u + k) % NU
                yield remote(qs.at[v], qr.at[g, u], q_s.at[g], q_r.at[0], (where, v))

    def f_copies():
        for k in range(1, NU):
            v = (u + k) % NU
            yield remote(kvs.at[v], kvr.at[u], f_s.at[0], f_r.at[0], (pi, v))

    for copy in q_copies():
        copy.start()
    for copy in f_copies():
        copy.start()

    w_order = ((("own", 0), ("own", 1), ("far", 0), ("own", 2), ("far", 1)), (("own", 2), ("own", 0), ("far", 2), ("own", 1)))

    def w_slot(origin, quarter):
        quarter = jnp.where(yl == 0, quarter, 3 - quarter)
        return wg.at[rows(origin * 2 * HD + c * HD + quarter * 32, 32), :]

    def w_piece(direction, k, at):
        whose, quarter = w_order[direction][k]
        hops = (whose == "far") + at
        return w_slot((x + 4 - hops) % 4 if direction == 0 else (x + hops) % 4, quarter)

    def w_send(direction, k):
        slot = w_piece(direction, k, 0)
        remote(slot, slot, w_s.at[0], w_r.at[direction, k], (x_up, x_down)[direction]).start()

    def w_pass(slot):
        remote(slot, slot, w_s.at[0], wb_r.at[0], sibling).start()

    def w_arrived(direction, k):
        slot = w_piece(direction, k, 1)
        wait(slot, w_r.at[direction, k])
        w_pass(slot)

    w_origins = ((x + 3) % 4, (x + 1) % 4, (x + 2) % 4)

    def w_share(k):
        slot = w_slot(w_origins[k], 0)
        remote(slot, slot, w_s.at[0], wy_r.at[k], (other, u)).start()

    def w_shared(k):
        slot = w_slot(w_origins[k], 3)
        wait(slot, wy_r.at[k])
        w_pass(slot)

    w_local.wait()
    for k in range(2):
        for direction in range(2):
            w_send(direction, k)

    def w_step(n):
        if n == 12:
            for direction in range(2):
                w_arrived(direction, 0)
                w_send(direction, 2)
                w_send(direction, 3)
            w_share(0)
        if n == 17:
            w_arrived(0, 1)
            w_arrived(1, 1)
            w_send(0, 4)
            w_share(1)
        if n == 21:
            w_arrived(0, 2)
            w_arrived(1, 2)
        if n == 24:
            w_share(2)
            w_shared(0)
        if n == 26:
            w_arrived(0, 3)
            w_arrived(1, 3)
            w_shared(1)

    def assemble_queries():
        wait(qr, q_r.at[0])
        for g in range(2):
            got = [qr[g, v].astype(F32) for v in range(NU)]
            for h in range(2):
                q[h, pl.ds(g * GRP, GRP), :] = jnp.concatenate(
                    [t[h * TOK:(h + 1) * TOK] for t in got], axis=0
                ).astype(BF16)

    fresh_out = pltpu.make_async_copy(fresh, fresh_ref, local_sem.at[5])
    mixed_out = pltpu.make_async_copy(afin, mine_ref, local_sem.at[6])

    def assemble_fresh():
        wait(kvr, f_r.at[0])
        got = [kvr[v].astype(F32) for v in range(NU)]
        for kind in range(4):
            whole = jnp.concatenate([t[kind * TOK:(kind + 1) * TOK] for t in got], axis=0).astype(BF16)
            fr[kind, rows(c * GRP, GRP), :] = whole
            fresh[kind // 2, :, pl.ds(kind % 2 * HD, HD)] = whole
        fresh_out.start()
        wait(kv.at[:, rows(OWN + (1 - c) * GRP, GRP), :], own_r.at[0])
        for kind in range(4):
            fr[kind, rows((1 - c) * GRP, GRP), :] = kv[kind, rows(OWN + (1 - c) * GRP, GRP), :]

    def note_max(h, first, scores):
        count, width = scores.shape
        for r in range(0, count, BAND):
            span = pl.ds(first + r, BAND)
            best = m[h, span, :]
            for t in range(width // HD):
                best = jnp.maximum(best, scores[r:r + BAND, t * HD:(t + 1) * HD])
            m[h, span, :] = best

    def score(h, j, width):
        scores = lax.dot_general(q[h], kv[h, rows(j * 2 * PAIR, width), :], NT, preferred_element_type=F32)
        s[h, j, :, pl.ds(0, width)] = scores
        note_max(h, 0, scores)

    def score_own(h):
        for g, keys in ((0, fr.at[h]), (1, kv.at[h, pl.ds(OWN, PAIR)])):
            span = pl.ds(g * GRP, GRP)
            scores = lax.dot_general(q[h, span, :], keys[...], NT, preferred_element_type=F32)
            s[h, 3, span, pl.ds(PAIR, PAIR)] = scores
            note_max(h, g * GRP, scores)

    def weigh(h, j, first, width):
        for r in range(0, PAIR, BAND):
            span = pl.ds(r, BAND)
            most, total = top[h, span, :], None
            for t in range(first // HD, (first + width) // HD):
                keys = pl.ds(t * HD, HD)
                weight = jnp.exp2(s[h, j, span, keys] * SCALE - most)
                total = weight if total is None else total + weight
                p[h, j, span, keys] = weight.astype(BF16)
            l[h, span, :] += total

    def attend(h, j, width):
        acc[h] += jnp.dot(
            p[h, j, :, pl.ds(0, width)], kv[2 + h, rows(j * 2 * PAIR, width), :], preferred_element_type=F32
        )

    def attend_own(h):
        for g, values in ((0, fr.at[2 + h]), (1, kv.at[2 + h, pl.ds(OWN, PAIR)])):
            span = pl.ds(g * GRP, GRP)
            acc[h, span, :] += jnp.dot(p[h, 3, span, pl.ds(PAIR, PAIR)], values[...], preferred_element_type=F32)

    def arrived(phase, i):
        wait(kv.at[0, pl.ds(0, PAIR)], sib_r.at[turn_of(phase, i)])

    def for_heads(f):
        lax.fori_loop(0, 2, lambda h, _: (f(h), 0)[1], 0)

    def row_max(h):
        return jnp.broadcast_to(jnp.max(m[h], axis=1, keepdims=True) * SCALE, (PAIR, HD))

    def first_top():
        for h in range(2):
            top[h] = row_max(h)

    def next_top():
        for h in range(2):
            old, new = top[h], row_max(h)
            top[h] = new
            fix[h] = jnp.exp2(old - new)
            l[h] = l[h] * fix[h]

    def scale_acc(h):
        acc[h] = acc[h] * fix[h]

    lane = lax.broadcasted_iota(jnp.int32, (PAIR, HD), 1)

    def stat_copy():
        return remote(stat_out, stat_in, st_s.at[0], st_r.at[0], (other, u))

    def send_stats():
        packed = jnp.zeros((PAIR, HD), F32)
        for h in range(2):
            total = jnp.broadcast_to(jnp.sum(l[h], axis=1, keepdims=True), (PAIR, HD))
            l[h] = total
            packed = jnp.where(lane == 2 * h, top[h], packed)
            packed = jnp.where(lane == 2 * h + 1, total, packed)
        stat_out[...] = packed.T[:8]
        stat_copy().start()

    def take_stats():
        stat_copy().wait_recv()
        got = jnp.concatenate([stat_in[...], jnp.zeros((HD - 8, PAIR), F32)], axis=0).T
        got = jnp.concatenate([got[GRP:], got[:GRP]], axis=0)
        for h in range(2):
            their_top, total = got[:, 2 * h:2 * h + 1], got[:, 2 * h + 1:2 * h + 2]
            mine_top, mine_total = top[h], l[h]
            most = jnp.maximum(mine_top, their_top)
            own = jnp.exp2(mine_top - most)
            l[h] = own / (mine_total * own + total * jnp.exp2(their_top - most))

    def step(n):
        wait(kv.at[0, pl.ds(0, GRP), :], ring_r.at[n])

        if n < 26 - AHEAD:
            for copy in ring_copies(n + AHEAD):
                copy.start()

        if (n == 22) or (n == 23):
            for copy in ring_copies(n + 4):
                copy.start()

        if n % 2 == 1:
            for copy in sib_copies(n):
                copy.start()

        if n == 4:
            assemble_queries()

        if (n == 4) or (n == 10) or (n == 16):
            arrived(0, (n - 4) // 3)
            arrived(0, (n - 4) // 3 + 1)

        if (n == 4) or (n == 5) or (n == 10) or (n == 11) or (n == 16) or (n == 17):
            score(n % 2, (n - 4) // 6, 2 * PAIR)

        if n == 7:
            assemble_fresh()
            for_heads(score_own)

        if n == 22:
            arrived(0, 6)
            for_heads(lambda h: score(h, 3, PAIR))

        if n == 8:
            first_top()
            for_heads(lambda h: weigh(h, 3, PAIR, PAIR))

        if n == 18:
            next_top()
            for_heads(scale_acc)

        if n == 23:
            next_top()
            for_heads(lambda h: weigh(h, 3, 0, PAIR))

        if (n == 9) or (n == 12) or ((n >= 18) and (n <= 21)):
            weigh(int(n in (12, 19, 21)), 0 if n <= 12 else 1 if n <= 19 else 2, 0, 2 * PAIR)

        if n == 23:
            send_stats()

        if n == 13:
            for_heads(attend_own)

        if (n == 14) or (n == 24) or (n == 26):
            i = {14: 0, 24: 2, 26: 4}[n]
            arrived(1, i)
            arrived(1, i + 1)

        if (n == 14) or (n == 24) or (n == 26):
            for_heads(lambda h: attend(h, i // 2, 2 * PAIR))

        w_step(n)

    for n in range(2 * STEPS):
        step(n)
    take_stats()
    for_heads(scale_acc)

    order = [(False, 2), (True, 2), (False, 1), (False, 3), (True, 1), (True, 3), (False, 0), (True, 0)]

    def hand_out(part_):
        for same, dx in order:
            xt = (x + dx) % 4
            k = (0 if same else 4) + dx
            group = GRP if same == (part_ == 1) else 0
            tokens = rows(group + TOK * (4 * ((1 - yh) if part_ == 1 else yh) + xt), TOK, 8)
            osend[part_, k] = jnp.concatenate([acc[h, tokens, :] * l[h, tokens, :] for h in range(2)], axis=0).astype(BF16)
            slot = orecv.at[part_, yl * 4 + x]
            if same and dx == 0:
                pltpu.make_async_copy(osend.at[part_, k], slot, o_r.at[part_]).start()
            else:
                remote(
                    osend.at[part_, k], slot, o_s.at[0], o_r.at[part_], (pi if same else other, yh * 4 + xt)
                ).start()

    arrived(1, 6)
    for_heads(lambda h: attend(h, 3, PAIR))
    hand_out(1)
    hand_out(0)

    w_arrived(0, 4)
    w_shared(2)
    wait(wg.at[pl.ds(0, 3 * HD), :], wb_r.at[0])

    facing = (other, (1 - yh) * 4 + x)

    def collect(part_):
        wait(orecv.at[part_], o_r.at[part_])
        columns = []
        for sx in range(4):
            both = orecv[part_, sx].astype(F32) + orecv[part_, 4 + sx].astype(F32)
            columns += [both[:TOK], both[TOK:]]
        return jnp.concatenate(columns, axis=1).astype(BF16)

    att[...] = collect(1)

    def project_theirs(n, _):
        columns = pl.ds(pl.multiple_of(n * CHUNK, CHUNK), CHUNK)
        got = jnp.dot(att[...], wg[:, columns], preferred_element_type=F32)
        span = rows(n * HALF, HALF)
        bsend[span, :] = jnp.concatenate(
            [got[:, t * HD:(t + 1) * HD] for t in range(CHUNK // HD)], axis=0
        ).astype(BF16)
        remote(bsend.at[span, :], their_ref.at[span, :], b_s.at[0], b_r.at[0], facing).start()
        return 0

    lax.fori_loop(0, D // CHUNK, project_theirs, 0)
    att[...] = collect(0)

    def project_mine(n, _):
        columns = pl.ds(pl.multiple_of(n * CHUNK, CHUNK), CHUNK)
        afin[:, columns] = jnp.dot(att[...], wg[:, columns], preferred_element_type=F32)
        return 0

    lax.fori_loop(0, D // CHUNK, project_mine, 0)
    mixed_out.start()

    wait(kv.at[:, pl.ds(0, OWN), :], pass_s.at[0])
    wait(kv.at[:, mine, :], own_s.at[0])
    wait(qs.at[pl.ds(1, 7)], q_s.at[0])
    wait(qs, q_s.at[1])
    wait(kvs.at[pl.ds(1, 7)], f_s.at[0])
    wait(wg.at[pl.ds(0, 6 * HD), :], w_s.at[0])
    wait(stat_out, st_s.at[0])
    wait(osend.at[0, pl.ds(1, 7)], o_s.at[0])
    wait(osend.at[1, pl.ds(1, 7)], o_s.at[0])
    wait(bsend, b_s.at[0])
    wait(bsend, b_r.at[0])
    fresh_out.wait()
    mixed_out.wait()


def add_up(mine_ref, their_ref, fresh_in, mixed_ref, fresh_out):
    for n in range(D // CHUNK):
        theirs = their_ref[pl.ds(n * HALF, HALF), :].astype(F32)
        theirs = jnp.concatenate([theirs[t * TOK:(t + 1) * TOK] for t in range(CHUNK // HD)], axis=1)
        span = pl.ds(n * CHUNK, CHUNK)
        mixed_ref[:, span] = (mine_ref[:, span] + theirs).astype(BF16)
    fresh_out[...] = fresh_in[...]


def on_device(qkv, stale_kv, out_weight):
    vmem = pl.BlockSpec(memory_space=pltpu.VMEM)
    dma = pltpu.SemaphoreType.DMA
    anywhere = pl.BlockSpec(memory_space=pl.ANY)
    fresh = jax.ShapeDtypeStruct((2, GRP, 2 * HD), BF16)
    results = pl.pallas_call(
        kernel,
        out_shape=(
            jax.ShapeDtypeStruct((TOK, D), F32),
            jax.ShapeDtypeStruct((TOK * D // HD, HD), BF16),
            fresh,
        ),
        in_specs=[anywhere] * 3,
        out_specs=(anywhere,) * 3,
        scratch_shapes=[
            pltpu.VMEM((3, TOK, NU * 2 * HD), BF16),
            pltpu.VMEM((4, NZ * PAIR, HD), BF16),
            pltpu.VMEM((4, PAIR, HD), BF16),
            pltpu.VMEM((2, PAIR, HD), BF16),
            pltpu.VMEM((2, NZ // 2, PAIR, 2 * PAIR), F32),
            pltpu.VMEM((2, NZ // 2, PAIR, 2 * PAIR), BF16),
            pltpu.VMEM((2, PAIR, HD), F32),
            pltpu.VMEM((2, PAIR, HD), F32),
            pltpu.VMEM((2, PAIR, HD), F32),
            pltpu.VMEM((2, PAIR, HD), F32),
            pltpu.VMEM((2, PAIR, HD), F32),
            pltpu.VMEM((NU, 2 * TOK, HD), BF16),
            pltpu.VMEM((NU, 4 * TOK, HD), BF16),
            pltpu.VMEM((2, NU, 2 * TOK, HD), BF16),
            pltpu.VMEM((NU, 4 * TOK, HD), BF16),
            pltpu.VMEM((8 * HD, D), BF16),
            pltpu.VMEM((8, PAIR), F32),
            pltpu.VMEM((8, PAIR), F32),
            pltpu.VMEM((2, 8, 2 * TOK, HD), BF16),
            pltpu.VMEM((2, 8, 2 * TOK, HD), BF16),
            pltpu.VMEM((TOK, 8 * HD), BF16),
            pltpu.VMEM((TOK * D // HD, HD), BF16),
            pltpu.VMEM((TOK, D), F32),
            pltpu.VMEM((2, GRP, 2 * HD), BF16),
            dma((8,)), dma((2 * STEPS,)), dma((1,)), dma((STEPS,)), dma((1,)), dma((1,)),
            dma((2,)), dma((1,)), dma((1,)), dma((1,)), dma((1,)), dma((2, 5)), dma((1,)), dma((3,)),
            dma((1,)), dma((1,)), dma((1,)), dma((2,)), dma((1,)), dma((1,)),
        ],
        compiler_params=pltpu.CompilerParams(
            collective_id=0, has_side_effects=True, vmem_limit_bytes=62 * 2**20
        ),
    )(qkv, stale_kv, out_weight)
    return pl.pallas_call(
        add_up,
        out_shape=(jax.ShapeDtypeStruct((TOK, D), BF16), fresh),
        in_specs=[vmem] * 3,
        out_specs=(vmem, vmem),
    )(*results)


def solution(mesh):
    placed = (P(None, ("patch", "uly"), None), P(None, "patch", "uly"), P("uly", None))
    return jax.shard_map(
        on_device,
        mesh=mesh,
        in_specs=placed,
        out_specs=(P(("patch", "uly"), None), P(None, "patch", "uly")),
        check_vma=False,
    )
```

```python
import functools

import jax
import jax.numpy as jnp
from jax import lax
from jax.experimental import pallas as pl
from jax.experimental.pallas import tpu as pltpu
from jax.sharding import PartitionSpec as P

MESH = pl.DeviceIdType.MESH
HD = 128
NZ = 8
NU = 8
TOK = 40
GRP = 320
PAIR = 640
HALF = 160
BAND = 64
OWN = 7 * PAIR
D = 3072
STEPS = 14
SCALE = HD ** -0.5 * 1.4426950408889634
NT = (((1,), (1,)), ((), ()))
F32 = jnp.float32
BF16 = jnp.bfloat16
AHEAD = 6
CHUNK = 512


def rows(offset, size, unit=16):
    return pl.ds(pl.multiple_of(offset, unit), size)


def kernel(
    qkv_ref, stale_ref, w_ref, mine_ref, their_ref, fresh_ref,
    qkv, kv, fr, q, s, p, m, top, fix, l, acc, qs, kvs, qr, kvr, wg, stat_out, stat_in,
    osend, orecv, att, bsend, afin, fresh,
    local_sem, ring_r, pass_s, sib_r, own_s, own_r, q_s, q_r, f_s, f_r,
    w_s, w_r, wb_r, wy_r, st_s, st_r, o_s, o_r, b_s, b_r,
):
    pi, u = lax.axis_index("patch"), lax.axis_index("uly")
    z, yl, c = pi // 4, (pi // 2) % 2, pi % 2
    yh, x = u // 4, u % 4

    def patch(z_, yl_, c_):
        return z_ * 4 + yl_ * 2 + c_

    sibling = (patch(z, yl, 1 - c), u)
    up = (patch((z + 1) % NZ, yl, c), u)
    down = (patch((z + 7) % NZ, yl, c), u)
    x_up = (pi, yh * 4 + (x + 1) % 4)
    x_down = (pi, yh * 4 + (x + 3) % 4)
    other = patch(z, 1 - yl, c)

    barrier = pltpu.get_barrier_semaphore()
    everyone = [sibling, up, down]
    everyone += [(pi, (u + k) % NU) for k in range(1, NU)]
    everyone += [(other, (u + k) % NU) for k in range(NU)]
    for device in everyone:
        pl.semaphore_signal(barrier, inc=1, device_id=device, device_id_type=MESH)

    def remote(src, dst, send, recv, device):
        return pltpu.make_async_remote_copy(
            src_ref=src, dst_ref=dst, send_sem=send, recv_sem=recv, device_id=device, device_id_type=MESH
        )

    mine = rows(OWN + c * GRP, GRP)
    def wait(ref, sem):
        pltpu.make_async_copy(ref, ref, sem).wait()

    qkv_in = pltpu.make_async_copy(qkv_ref, qkv, local_sem.at[7])
    locals_ = []
    for kind in range(4):
        locals_.append(pltpu.make_async_copy(
            stale_ref.at[kind // 2, :, pl.ds(kind % 2 * HD, HD)], kv.at[kind, mine, :], local_sem.at[kind]
        ))
    w_local = pltpu.make_async_copy(w_ref, wg.at[rows(x * 2 * HD, 2 * HD), :], local_sem.at[4])
    for copy in locals_:
        copy.start()
    qkv_in.start()
    w_local.start()

    for copy in locals_:
        copy.wait()
    pl.semaphore_wait(barrier, len(everyone))

    turns = ["Ka0", "Kb0", "Va0", "Ka1", "Kb1", "Vb0", "Ka2", "Kb2", "Va1", "Vb1", "Ka3", "Va2", "Vb2", "Va3"]

    def turn(n):
        phase, head, hop = turns[n // 2]
        return "KV".index(phase), 2 * int(hop) + "ab".index(head)

    def turn_of(phase, i):
        return turns.index("KV"[phase] + "ab"[i % 2] + str(i // 2))

    def place(hops, direction):
        return PAIR * {0: 7, 4: 6}.get(hops, 2 * hops - 2 + direction)

    def ring_copies(n):
        phase, i = turn(n)
        hop, head = i // 2, i % 2
        start = c * GRP + n % 2 * HALF
        for direction, device in ((0, up), (1, down)):
            kind = phase * 2 + (head if direction == 0 else 1 - head)
            yield remote(
                kv.at[kind, rows(place(hop, direction) + start, HALF), :],
                kv.at[kind, rows(place(hop + 1, direction) + start, HALF), :],
                pass_s.at[0], ring_r.at[n], device,
            )

    def sib_copies(n):
        phase, i = turn(n)
        hop, head = i // 2, i % 2
        for direction in range(2):
            kind = phase * 2 + (head if direction == 0 else 1 - head)
            slot = kv.at[kind, rows(place(hop + 1, direction) + c * GRP, GRP), :]
            yield remote(slot, slot, pass_s.at[0], sib_r.at[n // 2], sibling)

    for n in range(AHEAD):
        for copy in ring_copies(n):
            copy.start()
    own_sib = remote(kv.at[:, mine, :], kv.at[:, mine, :], own_s.at[0], own_r.at[0], sibling)
    own_sib.start()

    qkv_in.wait()
    for v in range(NU):
        parts = [
            qkv[i, :, pl.ds(v * 2 * HD + h * HD, HD)].astype(F32) for i in range(3) for h in range(2)
        ]
        qs[v] = jnp.concatenate(parts[:2], axis=0).astype(BF16)
        kvs[v] = jnp.concatenate(parts[2:], axis=0).astype(BF16)
    pltpu.make_async_copy(qs.at[u], qr.at[0, u], q_r.at[0]).start()
    pltpu.make_async_copy(kvs.at[u], kvr.at[u], f_r.at[0]).start()
    m[...] = jnp.full(m.shape, -jnp.inf, F32)
    l[...] = jnp.zeros(l.shape, F32)
    acc[...] = jnp.zeros(acc.shape, F32)

    def q_copies():
        for g, where in ((0, pi), (1, other)):
            for k in range(1 - g, NU):
                v = (u + k) % NU
                yield remote(qs.at[v], qr.at[g, u], q_s.at[g], q_r.at[0], (where, v))

    def f_copies():
        for k in range(1, NU):
            v = (u + k) % NU
            yield remote(kvs.at[v], kvr.at[u], f_s.at[0], f_r.at[0], (pi, v))

    for copy in q_copies():
        copy.start()

    w_order = ((("own", 0), ("far", 0), ("own", 1), ("own", 2), ("far", 1)), (("own", 0), ("own", 2), ("own", 1), ("far", 2)))

    def w_slot(origin, quarter):
        quarter = jnp.where(yl == 0, quarter, 3 - quarter)
        return wg.at[rows(origin * 2 * HD + c * HD + quarter * 32, 32), :]

    def w_piece(direction, k, at):
        whose, quarter = w_order[direction][k]
        hops = (whose == "far") + at
        return w_slot((x + 4 - hops) % 4 if direction == 0 else (x + hops) % 4, quarter)

    def w_send(direction, k):
        slot = w_piece(direction, k, 0)
        remote(slot, slot, w_s.at[0], w_r.at[direction, k], (x_up, x_down)[direction]).start()

    def w_pass(slot):
        remote(slot, slot, w_s.at[0], wb_r.at[0], sibling).start()

    def w_arrived(direction, k):
        slot = w_piece(direction, k, 1)
        wait(slot, w_r.at[direction, k])
        w_pass(slot)

    w_origins = ((x + 3) % 4, (x + 1) % 4, (x + 2) % 4)

    def w_share(k):
        slot = w_slot(w_origins[k], 0)
        remote(slot, slot, w_s.at[0], wy_r.at[k], (other, u)).start()

    def w_shared(k):
        slot = w_slot(w_origins[k], 3)
        wait(slot, wy_r.at[k])
        w_pass(slot)

    w_local.wait()
    for direction in range(2):
        w_send(direction, 0)
    for copy in f_copies():
        copy.start()

    def w_step(n):
        if n == 9:
            for direction in range(2):
                w_arrived(direction, 0)
                w_send(direction, 1)
                w_send(direction, 2)
            w_share(0)
            w_share(1)
        if n == 18:
            for direction in range(2):
                w_arrived(direction, 1)
                w_send(direction, 3)
            w_share(2)
        if n == 21:
            w_shared(0)
            w_shared(1)
        if n == 22:
            w_arrived(0, 2)
            w_arrived(1, 2)
            w_send(0, 4)
        if n == 27:
            w_arrived(0, 3)
            w_arrived(1, 3)
            w_shared(2)

    def assemble_queries():
        wait(qr, q_r.at[0])
        for g in range(2):
            got = [qr[g, v].astype(F32) for v in range(NU)]
            for h in range(2):
                q[h, pl.ds(g * GRP, GRP), :] = jnp.concatenate(
                    [t[h * TOK:(h + 1) * TOK] for t in got], axis=0
                ).astype(BF16)

    fresh_out = pltpu.make_async_copy(fresh, fresh_ref, local_sem.at[5])
    mixed_out = pltpu.make_async_copy(afin, mine_ref, local_sem.at[6])

    def assemble_fresh():
        wait(kvr, f_r.at[0])
        got = [kvr[v].astype(F32) for v in range(NU)]
        for kind in range(4):
            whole = jnp.concatenate([t[kind * TOK:(kind + 1) * TOK] for t in got], axis=0).astype(BF16)
            fr[kind, rows(c * GRP, GRP), :] = whole
            fresh[kind // 2, :, pl.ds(kind % 2 * HD, HD)] = whole
        fresh_out.start()
        wait(kv.at[:, rows(OWN + (1 - c) * GRP, GRP), :], own_r.at[0])
        for kind in range(4):
            fr[kind, rows((1 - c) * GRP, GRP), :] = kv[kind, rows(OWN + (1 - c) * GRP, GRP), :]

    def note_max(h, first, scores):
        count, width = scores.shape
        for r in range(0, count, BAND):
            span = pl.ds(first + r, BAND)
            best = m[h, span, :]
            for t in range(width // HD):
                best = jnp.maximum(best, scores[r:r + BAND, t * HD:(t + 1) * HD])
            m[h, span, :] = best

    def score(h, j, width):
        scores = lax.dot_general(q[h], kv[h, rows(j * 2 * PAIR, width), :], NT, preferred_element_type=F32)
        s[h, j, :, pl.ds(0, width)] = scores
        note_max(h, 0, scores)

    def score_own(h):
        for g, keys in ((0, fr.at[h]), (1, kv.at[h, pl.ds(OWN, PAIR)])):
            span = pl.ds(g * GRP, GRP)
            scores = lax.dot_general(q[h, span, :], keys[...], NT, preferred_element_type=F32)
            s[h, 3, span, pl.ds(PAIR, PAIR)] = scores
            note_max(h, g * GRP, scores)

    def weigh(h, j, first, width):
        for r in range(0, PAIR, BAND):
            span = pl.ds(r, BAND)
            most, total = top[h, span, :], None
            for t in range(first // HD, (first + width) // HD):
                keys = pl.ds(t * HD, HD)
                weight = jnp.exp2(s[h, j, span, keys] * SCALE - most)
                total = weight if total is None else total + weight
                p[h, j, span, keys] = weight.astype(BF16)
            l[h, span, :] += total

    def attend(h, j, width):
        acc[h] += jnp.dot(
            p[h, j, :, pl.ds(0, width)], kv[2 + h, rows(j * 2 * PAIR, width), :], preferred_element_type=F32
        )

    def attend_own(h):
        for g, values in ((0, fr.at[2 + h]), (1, kv.at[2 + h, pl.ds(OWN, PAIR)])):
            span = pl.ds(g * GRP, GRP)
            acc[h, span, :] += jnp.dot(p[h, 3, span, pl.ds(PAIR, PAIR)], values[...], preferred_element_type=F32)

    def arrived(phase, i):
        wait(kv.at[0, pl.ds(0, PAIR)], sib_r.at[turn_of(phase, i)])

    def for_heads(f):
        lax.fori_loop(0, 2, lambda h, _: (f(h), 0)[1], 0)

    def row_max(h):
        return jnp.broadcast_to(jnp.max(m[h], axis=1, keepdims=True) * SCALE, (PAIR, HD))

    def first_top():
        for h in range(2):
            top[h] = row_max(h)

    def next_top():
        for h in range(2):
            old, new = top[h], row_max(h)
            top[h] = new
            fix[h] = jnp.exp2(old - new)
            l[h] = l[h] * fix[h]

    def scale_acc(h):
        acc[h] = acc[h] * fix[h]

    lane = lax.broadcasted_iota(jnp.int32, (PAIR, HD), 1)

    def stat_copy():
        return remote(stat_out, stat_in, st_s.at[0], st_r.at[0], (other, u))

    def send_stats():
        packed = jnp.zeros((PAIR, HD), F32)
        for h in range(2):
            total = jnp.broadcast_to(jnp.sum(l[h], axis=1, keepdims=True), (PAIR, HD))
            l[h] = total
            packed = jnp.where(lane == 2 * h, top[h], packed)
            packed = jnp.where(lane == 2 * h + 1, total, packed)
        stat_out[...] = packed.T[:8]
        stat_copy().start()

    def take_stats():
        stat_copy().wait_recv()
        got = jnp.concatenate([stat_in[...], jnp.zeros((HD - 8, PAIR), F32)], axis=0).T
        got = jnp.concatenate([got[GRP:], got[:GRP]], axis=0)
        for h in range(2):
            their_top, total = got[:, 2 * h:2 * h + 1], got[:, 2 * h + 1:2 * h + 2]
            mine_top, mine_total = top[h], l[h]
            most = jnp.maximum(mine_top, their_top)
            own = jnp.exp2(mine_top - most)
            l[h] = own / (mine_total * own + total * jnp.exp2(their_top - most))

    def step(n):
        wait(kv.at[0, pl.ds(0, GRP), :], ring_r.at[n])

        if n < 26 - AHEAD:
            for copy in ring_copies(n + AHEAD):
                copy.start()

        if (n == 22) or (n == 23):
            for copy in ring_copies(n + 4):
                copy.start()

        if n % 2 == 1:
            for copy in sib_copies(n):
                copy.start()

        if n == 4:
            assemble_queries()

        if (n == 4) or (n == 10) or (n == 16):
            arrived(0, (n - 4) // 3)
            arrived(0, (n - 4) // 3 + 1)

        if (n == 4) or (n == 5) or (n == 10) or (n == 11) or (n == 16) or (n == 17):
            score(n % 2, (n - 4) // 6, 2 * PAIR)

        if n == 13:
            assemble_fresh()
            for_heads(score_own)

        if n == 22:
            arrived(0, 6)
            for_heads(lambda h: score(h, 3, PAIR))

        if n == 8:
            first_top()

        if n == 18:
            for_heads(attend_own)

        if n == 23:
            next_top()
            for_heads(lambda h: weigh(h, 3, 0, PAIR))

        if (n == 8) or (n == 9) or (n == 20) or (n == 21):
            weigh(n % 2, 0 if n <= 9 else 2, 0, 2 * PAIR)

        if n == 19:
            for_heads(lambda h: weigh(h, 1, 0, 2 * PAIR))

        if n == 23:
            send_stats()

        if (n == 14) or (n == 24) or (n == 27):
            i = {14: 0, 24: 2, 27: 4}[n]
            arrived(1, i)
            arrived(1, i + 1)

        if (n == 14) or (n == 24) or (n == 27):
            for_heads(lambda h: attend(h, i // 2, 2 * PAIR))

        if (n == 15) or (n == 18):
            next_top()
            for_heads(scale_acc)

        if n == 15:
            for_heads(lambda h: weigh(h, 3, PAIR, PAIR))

        w_step(n)

    for n in range(2 * STEPS):
        step(n)
    take_stats()
    for_heads(scale_acc)

    order = [(False, 2), (True, 2), (False, 1), (False, 3), (True, 1), (True, 3), (False, 0), (True, 0)]

    def hand_out(part_):
        for same, dx in order:
            xt = (x + dx) % 4
            k = (0 if same else 4) + dx
            group = GRP if same == (part_ == 1) else 0
            tokens = rows(group + TOK * (4 * ((1 - yh) if part_ == 1 else yh) + xt), TOK, 8)
            osend[part_, k] = jnp.concatenate([acc[h, tokens, :] * l[h, tokens, :] for h in range(2)], axis=0).astype(BF16)
            slot = orecv.at[part_, yl * 4 + x]
            if same and dx == 0:
                pltpu.make_async_copy(osend.at[part_, k], slot, o_r.at[part_]).start()
            else:
                remote(
                    osend.at[part_, k], slot, o_s.at[0], o_r.at[part_], (pi if same else other, yh * 4 + xt)
                ).start()

    def attend_last(half):
        def one(h):
            spans = [rows(g * GRP + half * HALF, HALF) for g in range(2)]
            weights = jnp.concatenate([p[h, 3, span, pl.ds(0, PAIR)] for span in spans], axis=0)
            got = jnp.dot(weights, kv[2 + h, pl.ds(6 * PAIR, PAIR), :], preferred_element_type=F32)
            for g, span in enumerate(spans):
                acc[h, span, :] += got[g * HALF:(g + 1) * HALF]

        for_heads(one)

    arrived(1, 6)
    attend_last(1 - yh)
    hand_out(1)
    attend_last(yh)
    hand_out(0)

    w_arrived(0, 4)
    wait(wg.at[pl.ds(0, 3 * HD), :], wb_r.at[0])

    facing = (other, (1 - yh) * 4 + x)

    def collect(part_):
        wait(orecv.at[part_], o_r.at[part_])
        columns = []
        for sx in range(4):
            both = orecv[part_, sx].astype(F32) + orecv[part_, 4 + sx].astype(F32)
            columns += [both[:TOK], both[TOK:]]
        return jnp.concatenate(columns, axis=1).astype(BF16)

    att[...] = collect(1)

    def project_theirs(n, _):
        columns = pl.ds(pl.multiple_of(n * CHUNK, CHUNK), CHUNK)
        got = jnp.dot(att[...], wg[:, columns], preferred_element_type=F32)
        span = rows(n * HALF, HALF)
        bsend[span, :] = jnp.concatenate(
            [got[:, t * HD:(t + 1) * HD] for t in range(CHUNK // HD)], axis=0
        ).astype(BF16)
        remote(bsend.at[span, :], their_ref.at[span, :], b_s.at[0], b_r.at[0], facing).start()
        return 0

    lax.fori_loop(0, D // CHUNK, project_theirs, 0)
    att[...] = collect(0)

    def project_mine(n, _):
        columns = pl.ds(pl.multiple_of(n * CHUNK, CHUNK), CHUNK)
        afin[:, columns] = jnp.dot(att[...], wg[:, columns], preferred_element_type=F32)
        return 0

    lax.fori_loop(0, D // CHUNK, project_mine, 0)
    mixed_out.start()

    wait(kv.at[:, pl.ds(0, OWN), :], pass_s.at[0])
    wait(kv.at[:, mine, :], own_s.at[0])
    wait(qs.at[pl.ds(1, 7)], q_s.at[0])
    wait(qs, q_s.at[1])
    wait(kvs.at[pl.ds(1, 7)], f_s.at[0])
    wait(wg.at[pl.ds(0, 6 * HD), :], w_s.at[0])
    wait(stat_out, st_s.at[0])
    wait(osend.at[0, pl.ds(1, 7)], o_s.at[0])
    wait(osend.at[1, pl.ds(1, 7)], o_s.at[0])
    wait(bsend, b_s.at[0])
    wait(bsend, b_r.at[0])
    fresh_out.wait()
    mixed_out.wait()


def add_up(mine_ref, their_ref, fresh_in, mixed_ref, fresh_out):
    for n in range(D // CHUNK):
        theirs = their_ref[pl.ds(n * HALF, HALF), :].astype(F32)
        theirs = jnp.concatenate([theirs[t * TOK:(t + 1) * TOK] for t in range(CHUNK // HD)], axis=1)
        span = pl.ds(n * CHUNK, CHUNK)
        mixed_ref[:, span] = (mine_ref[:, span] + theirs).astype(BF16)
    fresh_out[...] = fresh_in[...]


def on_device(qkv, stale_kv, out_weight):
    vmem = pl.BlockSpec(memory_space=pltpu.VMEM)
    dma = pltpu.SemaphoreType.DMA
    anywhere = pl.BlockSpec(memory_space=pl.ANY)
    fresh = jax.ShapeDtypeStruct((2, GRP, 2 * HD), BF16)
    results = pl.pallas_call(
        kernel,
        out_shape=(
            jax.ShapeDtypeStruct((TOK, D), F32),
            jax.ShapeDtypeStruct((TOK * D // HD, HD), BF16),
            fresh,
        ),
        in_specs=[anywhere] * 3,
        out_specs=(anywhere,) * 3,
        scratch_shapes=[
            pltpu.VMEM((3, TOK, NU * 2 * HD), BF16),
            pltpu.VMEM((4, NZ * PAIR, HD), BF16),
            pltpu.VMEM((4, PAIR, HD), BF16),
            pltpu.VMEM((2, PAIR, HD), BF16),
            pltpu.VMEM((2, NZ // 2, PAIR, 2 * PAIR), F32),
            pltpu.VMEM((2, NZ // 2, PAIR, 2 * PAIR), BF16),
            pltpu.VMEM((2, PAIR, HD), F32),
            pltpu.VMEM((2, PAIR, HD), F32),
            pltpu.VMEM((2, PAIR, HD), F32),
            pltpu.VMEM((2, PAIR, HD), F32),
            pltpu.VMEM((2, PAIR, HD), F32),
            pltpu.VMEM((NU, 2 * TOK, HD), BF16),
            pltpu.VMEM((NU, 4 * TOK, HD), BF16),
            pltpu.VMEM((2, NU, 2 * TOK, HD), BF16),
            pltpu.VMEM((NU, 4 * TOK, HD), BF16),
            pltpu.VMEM((8 * HD, D), BF16),
            pltpu.VMEM((8, PAIR), F32),
            pltpu.VMEM((8, PAIR), F32),
            pltpu.VMEM((2, 8, 2 * TOK, HD), BF16),
            pltpu.VMEM((2, 8, 2 * TOK, HD), BF16),
            pltpu.VMEM((TOK, 8 * HD), BF16),
            pltpu.VMEM((TOK * D // HD, HD), BF16),
            pltpu.VMEM((TOK, D), F32),
            pltpu.VMEM((2, GRP, 2 * HD), BF16),
            dma((8,)), dma((2 * STEPS,)), dma((1,)), dma((STEPS,)), dma((1,)), dma((1,)),
            dma((2,)), dma((1,)), dma((1,)), dma((1,)), dma((1,)), dma((2, 5)), dma((1,)), dma((3,)),
            dma((1,)), dma((1,)), dma((1,)), dma((2,)), dma((1,)), dma((1,)),
        ],
        compiler_params=pltpu.CompilerParams(
            collective_id=0, has_side_effects=True, vmem_limit_bytes=62 * 2**20
        ),
    )(qkv, stale_kv, out_weight)
    return pl.pallas_call(
        add_up,
        out_shape=(jax.ShapeDtypeStruct((TOK, D), BF16), fresh),
        in_specs=[vmem] * 3,
        out_specs=(vmem, vmem),
    )(*results)


def solution(mesh):
    placed = (P(None, ("patch", "uly"), None), P(None, "patch", "uly"), P("uly", None))
    return jax.shard_map(
        on_device,
        mesh=mesh,
        in_specs=placed,
        out_specs=(P(("patch", "uly"), None), P(None, "patch", "uly")),
        check_vma=False,
    )
```

```python
import functools

import jax
import jax.numpy as jnp
from jax import lax
from jax.experimental import pallas as pl
from jax.experimental.pallas import tpu as pltpu
from jax.sharding import PartitionSpec as P

MESH = pl.DeviceIdType.MESH
HD = 128
NZ = 8
NU = 8
TOK = 40
GRP = 320
PAIR = 640
HALF = 160
BAND = 64
OWN = 7 * PAIR
D = 3072
STEPS = 14
SCALE = HD ** -0.5 * 1.4426950408889634
NT = (((1,), (1,)), ((), ()))
F32 = jnp.float32
BF16 = jnp.bfloat16
AHEAD = 6
CHUNK = 512


def rows(offset, size, unit=16):
    return pl.ds(pl.multiple_of(offset, unit), size)


def kernel(
    qkv_ref, stale_ref, w_ref, mine_ref, their_ref, fresh_ref,
    qkv, kv, fr, q, s, p, m, top, fix, l, acc, qs, kvs, qr, kvr, wg, stat_out, stat_in,
    osend, orecv, att, bsend, afin, fresh,
    local_sem, ring_r, pass_s, sib_r, own_s, own_r, q_s, q_r, f_s, f_r,
    w_s, w_r, wb_r, wy_r, st_s, st_r, o_s, o_r, b_s, b_r,
):
    pi, u = lax.axis_index("patch"), lax.axis_index("uly")
    z, yl, c = pi // 4, (pi // 2) % 2, pi % 2
    yh, x = u // 4, u % 4

    def patch(z_, yl_, c_):
        return z_ * 4 + yl_ * 2 + c_

    sibling = (patch(z, yl, 1 - c), u)
    up = (patch((z + 1) % NZ, yl, c), u)
    down = (patch((z + 7) % NZ, yl, c), u)
    x_up = (pi, yh * 4 + (x + 1) % 4)
    x_down = (pi, yh * 4 + (x + 3) % 4)
    other = patch(z, 1 - yl, c)

    barrier = pltpu.get_barrier_semaphore()
    everyone = [sibling, up, down]
    everyone += [(pi, (u + k) % NU) for k in range(1, NU)]
    everyone += [(other, (u + k) % NU) for k in range(NU)]
    for device in everyone:
        pl.semaphore_signal(barrier, inc=1, device_id=device, device_id_type=MESH)

    def remote(src, dst, send, recv, device):
        return pltpu.make_async_remote_copy(
            src_ref=src, dst_ref=dst, send_sem=send, recv_sem=recv, device_id=device, device_id_type=MESH
        )

    mine = rows(OWN + c * GRP, GRP)
    def wait(ref, sem):
        pltpu.make_async_copy(ref, ref, sem).wait()

    qkv_in = pltpu.make_async_copy(qkv_ref, qkv, local_sem.at[7])
    locals_ = []
    for kind in range(4):
        locals_.append(pltpu.make_async_copy(
            stale_ref.at[kind // 2, :, pl.ds(kind % 2 * HD, HD)], kv.at[kind, mine, :], local_sem.at[kind]
        ))
    w_local = pltpu.make_async_copy(w_ref, wg.at[rows(x * 2 * HD, 2 * HD), :], local_sem.at[4])
    for copy in locals_:
        copy.start()
    qkv_in.start()
    w_local.start()

    for copy in locals_:
        copy.wait()
    pl.semaphore_wait(barrier, len(everyone))

    turns = ["Ka0", "Kb0", "Va0", "Ka1", "Kb1", "Vb0", "Ka2", "Kb2", "Va1", "Vb1", "Ka3", "Va2", "Vb2", "Va3"]

    def turn(n):
        phase, head, hop = turns[n // 2]
        return "KV".index(phase), 2 * int(hop) + "ab".index(head)

    def turn_of(phase, i):
        return turns.index("KV"[phase] + "ab"[i % 2] + str(i // 2))

    def place(hops, direction):
        return PAIR * {0: 7, 4: 6}.get(hops, 2 * hops - 2 + direction)

    def ring_copies(n):
        phase, i = turn(n)
        hop, head = i // 2, i % 2
        start = c * GRP + n % 2 * HALF
        for direction, device in ((0, up), (1, down)):
            kind = phase * 2 + (head if direction == 0 else 1 - head)
            yield remote(
                kv.at[kind, rows(place(hop, direction) + start, HALF), :],
                kv.at[kind, rows(place(hop + 1, direction) + start, HALF), :],
                pass_s.at[0], ring_r.at[n], device,
            )

    def sib_copies(n):
        phase, i = turn(n)
        hop, head = i // 2, i % 2
        for direction in range(2):
            kind = phase * 2 + (head if direction == 0 else 1 - head)
            slot = kv.at[kind, rows(place(hop + 1, direction) + c * GRP, GRP), :]
            yield remote(slot, slot, pass_s.at[0], sib_r.at[n // 2], sibling)

    for n in range(AHEAD):
        for copy in ring_copies(n):
            copy.start()
    own_sib = remote(kv.at[:, mine, :], kv.at[:, mine, :], own_s.at[0], own_r.at[0], sibling)
    own_sib.start()

    qkv_in.wait()
    for v in range(NU):
        parts = [
            qkv[i, :, pl.ds(v * 2 * HD + h * HD, HD)].astype(F32) for i in range(3) for h in range(2)
        ]
        qs[v] = jnp.concatenate(parts[:2], axis=0).astype(BF16)
        kvs[v] = jnp.concatenate(parts[2:], axis=0).astype(BF16)
    pltpu.make_async_copy(qs.at[u], qr.at[0, u], q_r.at[0]).start()
    pltpu.make_async_copy(kvs.at[u], kvr.at[u], f_r.at[0]).start()
    m[...] = jnp.full(m.shape, -jnp.inf, F32)
    l[...] = jnp.zeros(l.shape, F32)
    acc[...] = jnp.zeros(acc.shape, F32)

    def q_copies():
        for g, where in ((0, pi), (1, other)):
            for k in range(1 - g, NU):
                v = (u + k) % NU
                yield remote(qs.at[v], qr.at[g, u], q_s.at[g], q_r.at[0], (where, v))

    def f_copies():
        for k in range(1, NU):
            v = (u + k) % NU
            yield remote(kvs.at[v], kvr.at[u], f_s.at[0], f_r.at[0], (pi, v))

    for copy in q_copies():
        copy.start()

    w_order = ((("own", 0), ("far", 0), ("own", 1), ("own", 2), ("far", 1)), (("own", 0), ("own", 2), ("own", 1), ("far", 2)))

    def w_slot(origin, quarter):
        quarter = jnp.where(yl == 0, quarter, 3 - quarter)
        return wg.at[rows(origin * 2 * HD + c * HD + quarter * 32, 32), :]

    def w_piece(direction, k, at):
        whose, quarter = w_order[direction][k]
        hops = (whose == "far") + at
        return w_slot((x + 4 - hops) % 4 if direction == 0 else (x + hops) % 4, quarter)

    def w_send(direction, k):
        slot = w_piece(direction, k, 0)
        remote(slot, slot, w_s.at[0], w_r.at[direction, k], (x_up, x_down)[direction]).start()

    def w_pass(slot):
        remote(slot, slot, w_s.at[0], wb_r.at[0], sibling).start()

    def w_arrived(direction, k):
        slot = w_piece(direction, k, 1)
        wait(slot, w_r.at[direction, k])
        w_pass(slot)

    w_origins = ((x + 3) % 4, (x + 1) % 4, (x + 2) % 4)

    def w_share(k):
        slot = w_slot(w_origins[k], 0)
        remote(slot, slot, w_s.at[0], wy_r.at[k], (other, u)).start()

    def w_shared(k):
        slot = w_slot(w_origins[k], 3)
        wait(slot, wy_r.at[k])
        w_pass(slot)

    w_local.wait()
    for direction in range(2):
        w_send(direction, 0)
    for copy in f_copies():
        copy.start()

    def w_step(n):
        if n == 9:
            for direction in range(2):
                w_arrived(direction, 0)
                w_send(direction, 1)
                w_send(direction, 2)
            w_send(0, 3)
            w_share(0)
            w_share(1)
        if n == 18:
            for direction in range(2):
                w_arrived(direction, 1)
            w_send(1, 3)
            w_share(2)
        if n == 21:
            w_shared(0)
            w_shared(1)
        if n == 22:
            w_arrived(0, 2)
            w_arrived(1, 2)
            w_send(0, 4)
        if n == 27:
            w_arrived(0, 3)
            w_arrived(1, 3)
            w_shared(2)

    def assemble_queries():
        wait(qr, q_r.at[0])
        for g in range(2):
            got = [qr[g, v].astype(F32) for v in range(NU)]
            for h in range(2):
                q[h, pl.ds(g * GRP, GRP), :] = jnp.concatenate(
                    [t[h * TOK:(h + 1) * TOK] for t in got], axis=0
                ).astype(BF16)

    fresh_out = pltpu.make_async_copy(fresh, fresh_ref, local_sem.at[5])
    mixed_out = pltpu.make_async_copy(afin, mine_ref, local_sem.at[6])

    def assemble_fresh():
        wait(kvr, f_r.at[0])
        got = [kvr[v].astype(F32) for v in range(NU)]
        for kind in range(4):
            whole = jnp.concatenate([t[kind * TOK:(kind + 1) * TOK] for t in got], axis=0).astype(BF16)
            fr[kind, rows(c * GRP, GRP), :] = whole
            fresh[kind // 2, :, pl.ds(kind % 2 * HD, HD)] = whole
        fresh_out.start()
        wait(kv.at[:, rows(OWN + (1 - c) * GRP, GRP), :], own_r.at[0])
        for kind in range(4):
            fr[kind, rows((1 - c) * GRP, GRP), :] = kv[kind, rows(OWN + (1 - c) * GRP, GRP), :]

    def note_max(h, first, scores):
        count, width = scores.shape
        for r in range(0, count, BAND):
            span = pl.ds(first + r, BAND)
            best = m[h, span, :]
            for t in range(width // HD):
                best = jnp.maximum(best, scores[r:r + BAND, t * HD:(t + 1) * HD])
            m[h, span, :] = best

    def score(h, j, width):
        scores = lax.dot_general(q[h], kv[h, rows(j * 2 * PAIR, width), :], NT, preferred_element_type=F32)
        s[h, j, :, pl.ds(0, width)] = scores
        note_max(h, 0, scores)

    def score_own(h):
        for g, keys in ((0, fr.at[h]), (1, kv.at[h, pl.ds(OWN, PAIR)])):
            span = pl.ds(g * GRP, GRP)
            scores = lax.dot_general(q[h, span, :], keys[...], NT, preferred_element_type=F32)
            s[h, 3, span, pl.ds(PAIR, PAIR)] = scores
            note_max(h, g * GRP, scores)

    def weigh(h, j, first, width):
        for r in range(0, PAIR, BAND):
            span = pl.ds(r, BAND)
            most, total = top[h, span, :], None
            for t in range(first // HD, (first + width) // HD):
                keys = pl.ds(t * HD, HD)
                weight = jnp.exp2(s[h, j, span, keys] * SCALE - most)
                total = weight if total is None else total + weight
                p[h, j, span, keys] = weight.astype(BF16)
            l[h, span, :] += total

    def attend(h, j, width):
        acc[h] += jnp.dot(
            p[h, j, :, pl.ds(0, width)], kv[2 + h, rows(j * 2 * PAIR, width), :], preferred_element_type=F32
        )

    def attend_own(h):
        for g, values in ((0, fr.at[2 + h]), (1, kv.at[2 + h, pl.ds(OWN, PAIR)])):
            span = pl.ds(g * GRP, GRP)
            acc[h, span, :] += jnp.dot(p[h, 3, span, pl.ds(PAIR, PAIR)], values[...], preferred_element_type=F32)

    def arrived(phase, i):
        wait(kv.at[0, pl.ds(0, PAIR)], sib_r.at[turn_of(phase, i)])

    def for_heads(f):
        lax.fori_loop(0, 2, lambda h, _: (f(h), 0)[1], 0)

    def row_max(h):
        return jnp.broadcast_to(jnp.max(m[h], axis=1, keepdims=True) * SCALE, (PAIR, HD))

    def first_top():
        for h in range(2):
            top[h] = row_max(h)

    def next_top():
        for h in range(2):
            old, new = top[h], row_max(h)
            top[h] = new
            fix[h] = jnp.exp2(old - new)
            l[h] = l[h] * fix[h]

    def scale_acc(h):
        acc[h] = acc[h] * fix[h]

    lane = lax.broadcasted_iota(jnp.int32, (PAIR, HD), 1)

    def stat_copy():
        return remote(stat_out, stat_in, st_s.at[0], st_r.at[0], (other, u))

    def send_stats():
        packed = jnp.zeros((PAIR, HD), F32)
        for h in range(2):
            total = jnp.broadcast_to(jnp.sum(l[h], axis=1, keepdims=True), (PAIR, HD))
            l[h] = total
            packed = jnp.where(lane == 2 * h, top[h], packed)
            packed = jnp.where(lane == 2 * h + 1, total, packed)
        stat_out[...] = packed.T[:8]
        stat_copy().start()

    def take_stats():
        stat_copy().wait_recv()
        got = jnp.concatenate([stat_in[...], jnp.zeros((HD - 8, PAIR), F32)], axis=0).T
        got = jnp.concatenate([got[GRP:], got[:GRP]], axis=0)
        for h in range(2):
            their_top, total = got[:, 2 * h:2 * h + 1], got[:, 2 * h + 1:2 * h + 2]
            mine_top, mine_total = top[h], l[h]
            most = jnp.maximum(mine_top, their_top)
            own = jnp.exp2(mine_top - most)
            l[h] = own / (mine_total * own + total * jnp.exp2(their_top - most))

    def step(n):
        wait(kv.at[0, pl.ds(0, GRP), :], ring_r.at[n])

        if n < 26 - AHEAD:
            for copy in ring_copies(n + AHEAD):
                copy.start()

        if (n == 22) or (n == 23):
            for copy in ring_copies(n + 4):
                copy.start()

        if n % 2 == 1:
            for copy in sib_copies(n):
                copy.start()

        if n == 4:
            assemble_queries()

        if (n == 4) or (n == 10) or (n == 16):
            arrived(0, (n - 4) // 3)
            arrived(0, (n - 4) // 3 + 1)

        if (n == 4) or (n == 5) or (n == 10) or (n == 11) or (n == 16) or (n == 17):
            score(n % 2, (n - 4) // 6, 2 * PAIR)

        if n == 13:
            assemble_fresh()
            for_heads(score_own)

        if n == 22:
            arrived(0, 6)
            for_heads(lambda h: score(h, 3, PAIR))

        if n == 8:
            first_top()

        if n == 18:
            for_heads(attend_own)

        if n == 23:
            next_top()
            for_heads(lambda h: weigh(h, 3, 0, PAIR))

        if (n == 8) or (n == 9) or (n == 20) or (n == 21):
            weigh(n % 2, 0 if n <= 9 else 2, 0, 2 * PAIR)

        if n == 19:
            for_heads(lambda h: weigh(h, 1, 0, 2 * PAIR))

        if n == 23:
            send_stats()

        if (n == 14) or (n == 24) or (n == 27):
            i = {14: 0, 24: 2, 27: 4}[n]
            arrived(1, i)
            arrived(1, i + 1)

        if (n == 14) or (n == 24) or (n == 27):
            for_heads(lambda h: attend(h, i // 2, 2 * PAIR))

        if (n == 15) or (n == 18):
            next_top()
            for_heads(scale_acc)

        if n == 15:
            for_heads(lambda h: weigh(h, 3, PAIR, PAIR))

        w_step(n)

    for n in range(2 * STEPS):
        step(n)
    take_stats()
    for_heads(scale_acc)

    order = [(False, 2), (True, 2), (False, 1), (False, 3), (True, 1), (True, 3), (False, 0), (True, 0)]

    def hand_out(part_):
        for same, dx in order:
            xt = (x + dx) % 4
            k = (0 if same else 4) + dx
            group = GRP if same == (part_ == 1) else 0
            tokens = rows(group + TOK * (4 * ((1 - yh) if part_ == 1 else yh) + xt), TOK, 8)
            osend[part_, k] = jnp.concatenate([acc[h, tokens, :] * l[h, tokens, :] for h in range(2)], axis=0).astype(BF16)
            slot = orecv.at[part_, yl * 4 + x]
            if same and dx == 0:
                pltpu.make_async_copy(osend.at[part_, k], slot, o_r.at[part_]).start()
            else:
                remote(
                    osend.at[part_, k], slot, o_s.at[0], o_r.at[part_], (pi if same else other, yh * 4 + xt)
                ).start()

    def attend_last(half):
        def one(h):
            spans = [rows(g * GRP + half * HALF, HALF) for g in range(2)]
            weights = jnp.concatenate([p[h, 3, span, pl.ds(0, PAIR)] for span in spans], axis=0)
            got = jnp.dot(weights, kv[2 + h, pl.ds(6 * PAIR, PAIR), :], preferred_element_type=F32)
            for g, span in enumerate(spans):
                acc[h, span, :] += got[g * HALF:(g + 1) * HALF]

        for_heads(one)

    arrived(1, 6)
    attend_last(1 - yh)
    hand_out(1)
    attend_last(yh)
    hand_out(0)

    w_arrived(0, 4)
    wait(wg.at[pl.ds(0, 3 * HD), :], wb_r.at[0])

    facing = (other, (1 - yh) * 4 + x)

    def collect(part_):
        wait(orecv.at[part_], o_r.at[part_])
        columns = []
        for sx in range(4):
            both = orecv[part_, sx].astype(F32) + orecv[part_, 4 + sx].astype(F32)
            columns += [both[:TOK], both[TOK:]]
        return jnp.concatenate(columns, axis=1).astype(BF16)

    att[...] = collect(1)

    def project_theirs(n, _):
        columns = pl.ds(pl.multiple_of(n * CHUNK, CHUNK), CHUNK)
        got = jnp.dot(att[...], wg[:, columns], preferred_element_type=F32)
        span = rows(n * HALF, HALF)
        bsend[span, :] = jnp.concatenate(
            [got[:, t * HD:(t + 1) * HD] for t in range(CHUNK // HD)], axis=0
        ).astype(BF16)
        remote(bsend.at[span, :], their_ref.at[span, :], b_s.at[0], b_r.at[0], facing).start()
        return 0

    lax.fori_loop(0, D // CHUNK, project_theirs, 0)
    att[...] = collect(0)

    def project_mine(n, _):
        columns = pl.ds(pl.multiple_of(n * CHUNK, CHUNK), CHUNK)
        afin[:, columns] = jnp.dot(att[...], wg[:, columns], preferred_element_type=F32)
        return 0

    lax.fori_loop(0, D // CHUNK, project_mine, 0)
    mixed_out.start()

    wait(kv.at[:, pl.ds(0, OWN), :], pass_s.at[0])
    wait(kv.at[:, mine, :], own_s.at[0])
    wait(qs.at[pl.ds(1, 7)], q_s.at[0])
    wait(qs, q_s.at[1])
    wait(kvs.at[pl.ds(1, 7)], f_s.at[0])
    wait(wg.at[pl.ds(0, 6 * HD), :], w_s.at[0])
    wait(stat_out, st_s.at[0])
    wait(osend.at[0, pl.ds(1, 7)], o_s.at[0])
    wait(osend.at[1, pl.ds(1, 7)], o_s.at[0])
    wait(bsend, b_s.at[0])
    wait(bsend, b_r.at[0])
    fresh_out.wait()
    mixed_out.wait()


def add_up(mine_ref, their_ref, fresh_in, mixed_ref, fresh_out):
    for n in range(D // CHUNK):
        theirs = their_ref[pl.ds(n * HALF, HALF), :].astype(F32)
        theirs = jnp.concatenate([theirs[t * TOK:(t + 1) * TOK] for t in range(CHUNK // HD)], axis=1)
        span = pl.ds(n * CHUNK, CHUNK)
        mixed_ref[:, span] = (mine_ref[:, span] + theirs).astype(BF16)
    fresh_out[...] = fresh_in[...]


def on_device(qkv, stale_kv, out_weight):
    vmem = pl.BlockSpec(memory_space=pltpu.VMEM)
    dma = pltpu.SemaphoreType.DMA
    anywhere = pl.BlockSpec(memory_space=pl.ANY)
    fresh = jax.ShapeDtypeStruct((2, GRP, 2 * HD), BF16)
    results = pl.pallas_call(
        kernel,
        out_shape=(
            jax.ShapeDtypeStruct((TOK, D), F32),
            jax.ShapeDtypeStruct((TOK * D // HD, HD), BF16),
            fresh,
        ),
        in_specs=[anywhere] * 3,
        out_specs=(anywhere,) * 3,
        scratch_shapes=[
            pltpu.VMEM((3, TOK, NU * 2 * HD), BF16),
            pltpu.VMEM((4, NZ * PAIR, HD), BF16),
            pltpu.VMEM((4, PAIR, HD), BF16),
            pltpu.VMEM((2, PAIR, HD), BF16),
            pltpu.VMEM((2, NZ // 2, PAIR, 2 * PAIR), F32),
            pltpu.VMEM((2, NZ // 2, PAIR, 2 * PAIR), BF16),
            pltpu.VMEM((2, PAIR, HD), F32),
            pltpu.VMEM((2, PAIR, HD), F32),
            pltpu.VMEM((2, PAIR, HD), F32),
            pltpu.VMEM((2, PAIR, HD), F32),
            pltpu.VMEM((2, PAIR, HD), F32),
            pltpu.VMEM((NU, 2 * TOK, HD), BF16),
            pltpu.VMEM((NU, 4 * TOK, HD), BF16),
            pltpu.VMEM((2, NU, 2 * TOK, HD), BF16),
            pltpu.VMEM((NU, 4 * TOK, HD), BF16),
            pltpu.VMEM((8 * HD, D), BF16),
            pltpu.VMEM((8, PAIR), F32),
            pltpu.VMEM((8, PAIR), F32),
            pltpu.VMEM((2, 8, 2 * TOK, HD), BF16),
            pltpu.VMEM((2, 8, 2 * TOK, HD), BF16),
            pltpu.VMEM((TOK, 8 * HD), BF16),
            pltpu.VMEM((TOK * D // HD, HD), BF16),
            pltpu.VMEM((TOK, D), F32),
            pltpu.VMEM((2, GRP, 2 * HD), BF16),
            dma((8,)), dma((2 * STEPS,)), dma((1,)), dma((STEPS,)), dma((1,)), dma((1,)),
            dma((2,)), dma((1,)), dma((1,)), dma((1,)), dma((1,)), dma((2, 5)), dma((1,)), dma((3,)),
            dma((1,)), dma((1,)), dma((1,)), dma((2,)), dma((1,)), dma((1,)),
        ],
        compiler_params=pltpu.CompilerParams(
            collective_id=0, has_side_effects=True, vmem_limit_bytes=62 * 2**20
        ),
    )(qkv, stale_kv, out_weight)
    return pl.pallas_call(
        add_up,
        out_shape=(jax.ShapeDtypeStruct((TOK, D), BF16), fresh),
        in_specs=[vmem] * 3,
        out_specs=(vmem, vmem),
    )(*results)


def solution(mesh):
    placed = (P(None, ("patch", "uly"), None), P(None, "patch", "uly"), P("uly", None))
    return jax.shard_map(
        on_device,
        mesh=mesh,
        in_specs=placed,
        out_specs=(P(("patch", "uly"), None), P(None, "patch", "uly")),
        check_vma=False,
    )
```
